256 devices in a mesh: row: 16 (over y, z_lo, core), col: 16 (over z_hi, x).
Axes of the slice: x: 4, y: 4, z: 8 (z_hi: 4, z_lo: 2; z = z_hi * 2 + z_lo), core: 2. Of those that a mesh axis runs over, the one named last changes fastest.
Arguments:
- pair: bfloat16 [512, 512, 128], P('row', 'col'), may hold values from -6 to 6
- cotangent: bfloat16 [512, 512, 128], P('row', 'col'), may hold values from -6 to 6
- contact: int32 [4, 4], replicated, may hold values 0 or 1
- chain: int32 [512], replicated, may hold values from 0 to 3, never falling along the last dimension, each value on 1 to 256 neighbouring positions
- gain_in: float32 [128], replicated, may hold values from 0.1 to 1.9
- output_norm_gain: float32 [128], replicated, may hold values from 0.1 to 1.9
- w_in: bfloat16 [128, 512], replicated, may hold values from -0.5 to 0.5
- w_gate: bfloat16 [128, 128], replicated, may hold values from -0.5 to 0.5
- w_out: bfloat16 [128, 128], replicated, may hold values from -0.5 to 0.5
Outputs:
- update: bfloat16 [512, 512, 128], P('row', 'col')
- grad_pair: float32 [512, 512, 128], P('row', 'col')
- grad_w_in: float32 [128, 512], replicated
- grad_w_gate: float32 [128, 128], replicated
- grad_w_out: float32 [128, 128], replicated
- grad_gain_in: float32 [128], replicated
- output_norm_gain_gradient: float32 [128], replicated
The draws below stay inside these ranges and needn't reach their ends.
All inputs are finite; a program needn't handle non-finite values.
Results may differ from the reference program's by a relative error of at most 0.014.
Values may be sent and summed in bfloat16 or wider, within the bound.
No kernel may reach another device: no remote copies, remote signals or barrier semaphores. Data moves between devices by JAX's collectives and lax.ppermute only.
A program may use at most 128 MiB of HBM per device.

```python
import math
import jax
import jax.numpy as jnp
import numpy as np
from jax import lax

C = 128
H = 128
BLOCK = 128
CROP = 512
NB = 4


def touch_ends(array, key, low, top_value):
    extent = array.shape
    spot = [jax.random.randint(jax.random.fold_in(key, axis), (), 0, extent[axis]) for axis in range(len(extent))]
    array = array.at[tuple(spot)].set(low)
    longest = extent.index(max(extent))
    spot[longest] = (spot[longest] + 1) % extent[longest]
    return array.at[tuple(spot)].set(top_value)


def block_levels(own_key, extent, cuts, least, top_value):
    def one(dim, blocks):
        heights = jax.random.uniform(jax.random.fold_in(jax.random.fold_in(own_key, 6), dim), (blocks,), jnp.float32, least / len(cuts), top_value / len(cuts))
        return jnp.repeat(jnp.exp(heights), extent[dim] // blocks).reshape((-1,) + (1,) * (len(extent) - dim - 1))

    level = one(*cuts[0])
    for cut in cuts[1:]:
        level = level * one(*cut)
    return level


def profile(count, total, most, lean):
    loads = [(1 << 20) // math.isqrt(standing ** lean) + 1 for standing in range(2, count + 1)]
    rest, holding = total - most - (count - 1), [1] * (count - 1)
    while rest > 0:
        candidates = [i for i in range(count - 1) if holding[i] < most]
        whole, remaining = sum([loads[i] for i in candidates]), rest
        for i in candidates:
            more = min(most - holding[i], max(1, remaining * loads[i] // whole), rest)
            holding[i] = holding[i] + more
            rest = rest - more
    return np.array([most] + holding)


def uneven(key, number_of, total, limit, slope):
    if number_of == 2:
        one = jax.random.randint(key, (), max(1, total - limit), min(limit, total - 1) + 1)
        return jnp.stack([one, total - one])
    lengths = jnp.asarray(profile(number_of, total, limit, slope), jnp.int32)
    couples = (number_of - 1) // 2
    donor, sink = lengths[1:1 + 2 * couples:2], lengths[2:2 + 2 * couples:2]
    slack = jnp.minimum(donor - 1, limit - sink)
    shifted = jax.random.randint(jax.random.fold_in(key, 1), (couples,), 0, 1 << 20) % (slack + 1)
    lengths = lengths.at[1:1 + 2 * couples:2].set(donor - shifted).at[2:2 + 2 * couples:2].set(sink + shifted)
    return lengths[jax.random.permutation(jax.random.fold_in(key, 2), number_of)]


def normal_values(rng, dims, width, bound, pieces=(), dtype=jnp.bfloat16):
    array = width * jax.random.normal(rng, dims, jnp.float32)
    if pieces:
        array = array * block_levels(rng, dims, pieces, -0.22, 0.18)
    return jnp.clip(array, -bound, bound).astype(dtype)


def setup_inputs(seed: int = 0) -> dict:
    key_list = jax.random.split(jax.random.key(seed), 10)
    return {
        "pair": normal_values(key_list[0], (CROP, CROP, C), 1.0, 6.0, ((0, 16), (1, 16))),
        "cotangent": normal_values(key_list[1], (CROP, CROP, C), 1.0, 6.0, ((0, 16), (1, 16))),
        "contact": touch_ends((jax.random.randint(key_list[2], (NB, NB), 0, 2) < 1).astype(jnp.int32), jax.random.fold_in(key_list[2], 1), 0, 1),
        "chain": jnp.searchsorted(jnp.cumsum(uneven(key_list[3], 4, CROP, CROP // 2, 2)), jnp.arange(CROP), side="right").astype(jnp.int32),
        "gain_in": jnp.clip(1.0 + 0.18 * jax.random.normal(key_list[4], (C,), jnp.float32), 0.1, 1.9),
        "output_norm_gain": jnp.clip(1.0 + 0.18 * jax.random.normal(key_list[5], (H,), jnp.float32), 0.1, 1.9),
        "w_in": normal_values(key_list[6], (C, 4 * H), C ** -0.5, 0.5),
        "w_gate": normal_values(key_list[7], (C, C), C ** -0.5, 0.5),
        "w_out": normal_values(key_list[8], (H, C), H ** -0.5, 0.5),
    }


EPS = 1e-05
HIGH = lax.Precision.HIGHEST

def normalized_product(values):
    mean = lax.optimization_barrier(jnp.mean(values, axis=-1, keepdims=True))
    centred = values - mean
    rstd = lax.rsqrt(lax.optimization_barrier(jnp.mean(centred * centred, axis=-1, keepdims=True)) + EPS)
    return (centred * rstd, rstd)

def norm_backward_step(dnorm, nhat, rstd):
    first = lax.optimization_barrier(jnp.mean(dnorm, axis=-1, keepdims=True))
    second = lax.optimization_barrier(jnp.mean(dnorm * nhat, axis=-1, keepdims=True))
    return rstd * (dnorm - first - nhat * second)

def project_in(pair, gain_in, w_in, mask, hidden):
    nhat, rstd = normalized_product(pair.astype(jnp.float32))
    normed = (nhat * gain_in).astype(jnp.bfloat16)
    proj = jnp.einsum('pqc,cd->pqd', normed, w_in, preferred_element_type=jnp.float32)
    weight = mask[..., None]
    sig_a = jax.nn.sigmoid(proj[..., hidden:2 * hidden])
    sig_b = jax.nn.sigmoid(proj[..., 3 * hidden:])
    left = (sig_a * proj[..., :hidden] * weight).astype(jnp.bfloat16)
    right = (sig_b * proj[..., 2 * hidden:3 * hidden] * weight).astype(jnp.bfloat16)
    return (nhat, rstd, normed, proj, left, right)

def project_back(grad_left, grad_right, normed, proj, mask, w_in, hidden):
    weight = mask[..., None]
    fleft = grad_left.astype(jnp.float32) * weight
    fright = grad_right.astype(jnp.float32) * weight
    val_a = proj[..., :hidden]
    sig_a = jax.nn.sigmoid(proj[..., hidden:2 * hidden])
    val_b = proj[..., 2 * hidden:3 * hidden]
    sig_b = jax.nn.sigmoid(proj[..., 3 * hidden:])
    dproj = jnp.concatenate([fleft * sig_a, fleft * val_a * sig_a * (1.0 - sig_a), fright * sig_b, fright * val_b * sig_b * (1.0 - sig_b)], axis=-1)
    grad_w = jnp.einsum('pqc,pqd->cd', normed.astype(jnp.float32), dproj, precision=HIGH)
    dnormed = jnp.einsum('pqd,cd->pqc', dproj, w_in.astype(jnp.float32), precision=HIGH)
    return (dnormed, grad_w)

def output_pass(triangle_product, normed, cotangent, output_norm_gain, w_gate, w_out):
    gate = jax.nn.sigmoid(jnp.einsum('pqc,cd->pqd', normed, w_gate, preferred_element_type=jnp.float32))
    centred_scaled_input, input_reciprocal_deviation = normalized_product(triangle_product)
    input_normed_rows = (centred_scaled_input * output_norm_gain).astype(jnp.bfloat16)
    outp = jnp.einsum('pqh,hc->pqc', input_normed_rows, w_out, preferred_element_type=jnp.float32)
    update = (gate * outp).astype(jnp.bfloat16)
    dyf = cotangent.astype(jnp.float32)
    dout = dyf * gate
    dgpre = dyf * outp * gate * (1.0 - gate)
    grad_w_out = jnp.einsum('pqh,pqc->hc', input_normed_rows.astype(jnp.float32), dout, precision=HIGH)
    normed_input_gradient = jnp.einsum('pqc,hc->pqh', dout, w_out.astype(jnp.float32), precision=HIGH)
    output_norm_gain_gradient = lax.optimization_barrier(jnp.sum(normed_input_gradient * centred_scaled_input, axis=(0, 1)))
    product_gradient = norm_backward_step(normed_input_gradient * output_norm_gain, centred_scaled_input, input_reciprocal_deviation).astype(jnp.bfloat16)
    grad_w_gate = jnp.einsum('pqc,pqd->cd', normed.astype(jnp.float32), dgpre, precision=HIGH)
    dnormed = jnp.einsum('pqd,cd->pqc', dgpre, w_gate.astype(jnp.float32), precision=HIGH)
    return (update, product_gradient, dnormed, grad_w_out, output_norm_gain_gradient, grad_w_gate)

def reference(pair, cotangent, contact, chain, gain_in, output_norm_gain, w_in, w_gate, w_out):
    hidden = w_out.shape[0]
    blocks = (jnp.arange(CROP) // BLOCK).astype(jnp.int32)
    listed = contact[blocks[None, :], blocks[:, None]].astype(jnp.float32)
    same = (chain[:, None] == chain[None, :]).astype(jnp.float32)
    mask = jnp.maximum(listed, same)
    nhat, rstd, normed, proj, left, right = project_in(pair, gain_in, w_in, mask, hidden)
    triangle_product = jnp.einsum('kih,kjh->ijh', left.astype(jnp.float32), right.astype(jnp.float32), precision=HIGH)
    update, product_gradient, dnorm_out, grad_w_out, output_norm_gain_gradient, grad_w_gate = output_pass(triangle_product, normed, cotangent, output_norm_gain, w_gate, w_out)
    dpf = product_gradient.astype(jnp.float32)
    grad_right = jnp.einsum('kih,ijh->kjh', left.astype(jnp.float32), dpf, precision=HIGH).astype(jnp.bfloat16)
    grad_left = jnp.einsum('qjh,kjh->kqh', dpf, right.astype(jnp.float32), precision=HIGH).astype(jnp.bfloat16)
    dnorm_in, grad_w_in = project_back(grad_left, grad_right, normed, proj, mask, w_in, hidden)
    dnormed = dnorm_out + dnorm_in
    grad_gain_in = lax.optimization_barrier(jnp.sum(dnormed * nhat, axis=(0, 1)))
    grad_pair = norm_backward_step(dnormed * gain_in, nhat, rstd)
    return (update, grad_pair, grad_w_in, grad_w_gate, grad_w_out, grad_gain_in, output_norm_gain_gradient)
```

```python
import jax
import jax.numpy as jnp
from jax import lax
from jax.experimental import pallas as pl
from jax.experimental.pallas import tpu as pltpu
from jax.sharding import PartitionSpec as P


BLOCK = 128
EPS = 1e-05
F32 = jnp.float32
BF16 = jnp.bfloat16
AXES = ("row", "col")
VMEM_LIMIT = 48 * 1024 * 1024


def dot(x, y, dims):
    return lax.dot_general(x, y, (dims, ((), ())), preferred_element_type=F32)


NN = ((1,), (0,))
NT = ((1,), (1,))
TN = ((0,), (0,))


def norm_rows(values, axis):
    centred = values - jnp.mean(values, axis=axis, keepdims=True)
    rstd = lax.rsqrt(jnp.mean(centred * centred, axis=axis, keepdims=True) + EPS)
    return centred * rstd, rstd


def norm_back(e, nhat, rstd, axis):
    first = jnp.mean(e, axis=axis, keepdims=True)
    second = jnp.mean(e * nhat, axis=axis, keepdims=True)
    return rstd * (e - first - nhat * second)


def swap_segments(v):
    lane = lax.broadcasted_iota(jnp.int32, v[0].shape, 1)
    low = lane < 64
    even = (lane // 32) % 2 == 0
    w = [None] * 4
    for m in range(2):
        w[m] = jnp.where(low, v[m], pltpu.roll(v[m + 2], 64, 1))
        w[m + 2] = jnp.where(low, pltpu.roll(v[m], 64, 1), v[m + 2])
    u = [None] * 4
    for m in (0, 2):
        u[m] = jnp.where(even, w[m], pltpu.roll(w[m + 1], 32, 1))
        u[m + 1] = jnp.where(even, pltpu.roll(w[m], 96, 1), w[m + 1])
    return u


def group(ref, t):
    return ref[:, t].reshape(128, 128)


def project_kernel(pair, mask, gain, w_t, chunks, zn_out, scratch):
    for s in range(2):
        for half in range(4):
            t = 4 * s + half
            nhat, _ = norm_rows(group(pair, t).astype(F32), 1)
            zn = (nhat * gain[...]).astype(BF16)
            zn_out[t] = zn
            proj = dot(w_t[...], zn, NT)
            weight = mask[t : t + 1, :]
            scratch[:, half, :] = jax.nn.sigmoid(proj[128:256]) * proj[:128] * weight
            scratch[:, 4 + half, :] = jax.nn.sigmoid(proj[384:]) * proj[256:384] * weight
        chunks[:, s] = scratch[...].astype(BF16)


def product_kernel(got, x_out, left_out, right_out, rows_a, rows_b):
    sub = lax.broadcasted_iota(jnp.int32, (16, 8, 128), 1) < 4
    for hi in range(4):
        u = swap_segments([got[:, hi, lo].astype(F32).reshape(128, 128) for lo in range(4)])
        for m in range(4):
            block = u[m].reshape(16, 8, 128)
            swapped = jnp.concatenate([block[:, 4:], block[:, :4]], axis=1)
            rows, lanes = pl.ds(128 * m, 128), pl.ds(128 * hi, 128)
            rows_a[rows, lanes] = jnp.where(sub, block, 0.0).reshape(128, 128).astype(BF16)
            right_out[rows, lanes] = jnp.where(sub, swapped, 0.0).reshape(128, 128).astype(BF16)
            left_out[rows, lanes] = jnp.where(sub, 0.0, swapped).reshape(128, 128).astype(BF16)
    x = dot(rows_a[...], right_out[...], TN)
    rows_b[...] = x.reshape(16, 4, 8, 512)
    for hi in range(4):
        lanes = pl.ds(128 * hi, 128)
        u = swap_segments([rows_b[:, m, :, lanes].reshape(128, 128) for m in range(4)])
        for lo in range(4):
            x_out[:, hi, lo] = u[lo].reshape(16, 8, 128).astype(BF16)


def output_kernel(got, zn_in, cot, w_gate, w_out, gain, update, dx_out, dzn, grads, gain_sum, x_all, dx_all):
    x_all[...] = got[:, 0].astype(F32) + got[:, 1].astype(F32)
    for t in range(8):
        xhat, xrstd = norm_rows(x_all[:, t, :], 0)
        xn = (xhat * gain[...]).astype(BF16)
        outp = dot(xn, w_out[...], TN)
        zn = zn_in[t]
        gate = jax.nn.sigmoid(dot(zn, w_gate[...], NN))
        update[:, t] = (gate * outp).astype(BF16).reshape(4, 32, 128)
        dy = group(cot, t).astype(F32)
        dout = (dy * gate).astype(BF16)
        dgpre = (dy * outp * gate * (1.0 - gate)).astype(BF16)
        part_out = dot(xn, dout, NN)
        part_gate = dot(zn, dgpre, TN)
        dxn = dot(w_out[...], dout, NT)
        part_gain = dxn * xhat
        dx_all[:, t, :] = norm_back(dxn * gain[...], xhat, xrstd, 0)
        dzn[t] = dot(dgpre, w_gate[...], NT)
        if t == 0:
            grads[0:128] = part_out
            grads[128:256] = part_gate
            gain_sum[...] = part_gain
        else:
            grads[0:128] += part_out
            grads[128:256] += part_gate
            gain_sum[...] += part_gain
    dx = dx_all[...].astype(BF16)
    dx_out[:, 0] = dx
    dx_out[:, 1] = dx


def back_product_kernel(got, left, right, out, dx_rows, d_rows):
    for hi in range(4):
        u = swap_segments([got[:, hi, lo].astype(F32).reshape(128, 128) for lo in range(4)])
        for m in range(4):
            dx_rows[:, m, :, pl.ds(128 * hi, 128)] = u[m].reshape(16, 8, 128)
    dx = dx_rows[...].reshape(512, 512).astype(BF16)
    d_rows[...] = dot(right[...], dx, NT) + dot(left[...], dx, NN)
    for hi in range(4):
        lanes = pl.ds(128 * hi, 128)
        u = swap_segments([d_rows[pl.ds(128 * m, 128), lanes] for m in range(4)])
        for lo in range(4):
            out[:, hi, lo] = u[lo].reshape(16, 8, 128).astype(BF16)


def input_kernel(got, pair, mask, gain, w_t, dzn_in, grad_pair, grads, gain_sum, d_all):
    for s in range(2):
        d_all[...] = got[:, s].astype(F32)
        for half in range(4):
            t = 4 * s + half
            nhat, rstd = norm_rows(group(pair, t).astype(F32), 1)
            zn = (nhat * gain[...]).astype(BF16)
            proj = dot(w_t[...], zn, NT)
            weight = mask[t : t + 1, :]
            fa = d_all[:, half, :] * weight
            fb = d_all[:, 4 + half, :] * weight
            sa = jax.nn.sigmoid(proj[128:256])
            sb = jax.nn.sigmoid(proj[384:])
            da, db = fa * sa, fb * sb
            dproj = jnp.concatenate(
                [da, da * proj[:128] * (1.0 - sa), db, db * proj[256:384] * (1.0 - sb)], axis=0
            ).astype(BF16)
            part = dot(dproj, zn, NN)
            dzn = dot(dproj, w_t[...], TN) + dzn_in[t]
            part_gain = dzn * nhat
            grad_pair[:, t] = norm_back(dzn * gain[...], nhat, rstd, 1).reshape(4, 32, 128)
            if t == 0:
                grads[...] = part
                gain_sum[...] = part_gain
            else:
                grads[...] += part
                gain_sum[...] += part_gain


def call(kernel, outs, scratch, flops):
    return pl.pallas_call(
        kernel,
        out_shape=[jax.ShapeDtypeStruct(shape, dtype) for shape, dtype in outs],
        scratch_shapes=[pltpu.VMEM(shape, dtype) for shape, dtype in scratch],
        compiler_params=pltpu.CompilerParams(vmem_limit_bytes=VMEM_LIMIT),
        cost_estimate=pl.CostEstimate(flops=flops, bytes_accessed=2000000, transcendentals=0),
    )


def exchange(chunks):
    shape = chunks.shape
    flat = chunks.reshape((256,) + shape[-2:])
    return lax.all_to_all(flat, AXES, 0, 0, tiled=True)


def on_device(pair, cotangent, contact, chain, gain_in, output_norm_gain, w_in, w_gate, w_out):
    row_start = lax.axis_index("row") * 32
    col_start = lax.axis_index("col") * 32
    chain_row = lax.dynamic_slice_in_dim(chain, row_start, 32).reshape(4, 8).T
    chain_col = lax.dynamic_slice_in_dim(chain, col_start, 32)
    listed = contact[col_start // BLOCK, row_start // BLOCK] == 1
    mask = (listed | (chain_row[:, :, None] == chain_col[None, None, :])).astype(F32).reshape(8, 128)
    pair4 = pair.reshape(4, 8, 32, 128)
    cot4 = cotangent.reshape(4, 8, 32, 128)
    gain_row = gain_in.reshape(1, 128)
    gain_col = jnp.broadcast_to(output_norm_gain[:, None], (128, 128))
    w_t = w_in.T

    chunks, zn = call(
        project_kernel,
        [((128, 2, 8, 128), BF16), ((8, 128, 128), BF16)],
        [((128, 8, 128), F32)],
        134217728,
    )(pair4, mask, gain_row, w_t)
    got = exchange(chunks).reshape(16, 4, 4, 8, 128)
    x_chunks, left, right = call(
        product_kernel,
        [((16, 4, 4, 8, 128), BF16), ((512, 512), BF16), ((512, 512), BF16)],
        [((512, 512), BF16), ((16, 4, 8, 512), F32)],
        268435456,
    )(got)
    got = exchange(x_chunks).reshape(128, 2, 8, 128)
    update, dx_chunks, dzn, grads_early, gain_part = call(
        output_kernel,
        [
            ((4, 8, 32, 128), BF16),
            ((128, 2, 8, 128), BF16),
            ((8, 128, 128), F32),
            ((256, 128), F32),
            ((128, 128), F32),
        ],
        [((128, 8, 128), F32), ((128, 8, 128), F32)],
        201326592,
    )(got, zn, cot4, w_gate, w_out, gain_col)
    got = exchange(dx_chunks).reshape(16, 4, 4, 8, 128)
    (d_chunks,) = call(
        back_product_kernel,
        [((16, 4, 4, 8, 128), BF16)],
        [((16, 4, 8, 512), F32), ((512, 512), F32)],
        536870912,
    )(got, left, right)
    got = exchange(d_chunks).reshape(128, 2, 8, 128)
    grad_pair, grads_late, gain_in_part = call(
        input_kernel,
        [((4, 8, 32, 128), F32), ((512, 128), F32), ((128, 128), F32)],
        [((128, 8, 128), F32)],
        402653184,
    )(got, pair4, mask, gain_row, w_t, dzn)

    gains = jnp.zeros((256, 128), F32)
    gains = gains.at[0].set(jnp.sum(gain_in_part, axis=0)).at[1].set(jnp.sum(gain_part, axis=1))
    parts = jnp.stack([grads_late[:256], grads_late[256:], grads_early, gains], axis=1)
    parts = lax.all_to_all(parts.astype(BF16), AXES, 0, 0, tiled=True)
    total = jnp.sum(parts.astype(F32), axis=0)
    total = jnp.broadcast_to(total.astype(BF16)[None], (256, 4, 128))
    total = lax.all_to_all(total, AXES, 0, 0, tiled=True).astype(F32)
    grad_w_in = jnp.concatenate([total[:, 0], total[:, 1]], axis=0).T
    return (
        update.reshape(32, 32, 128),
        grad_pair.reshape(32, 32, 128),
        grad_w_in,
        total[128:, 2],
        total[:128, 2],
        total[0, 3],
        total[1, 3],
    )


def solution(mesh):
    return jax.shard_map(
        on_device,
        mesh=mesh,
        in_specs=(P("row", "col", None), P("row", "col", None), P(), P(), P(), P(), P(), P(), P()),
        out_specs=(P("row", "col", None), P("row", "col", None), P(), P(), P(), P(), P()),
        check_vma=False,
    )
```

```python
import jax
import jax.numpy as jnp
from jax import lax
from jax.experimental import pallas as pl
from jax.experimental.pallas import tpu as pltpu
from jax.sharding import PartitionSpec as P


BLOCK = 128
EPS = 1e-05
F32 = jnp.float32
BF16 = jnp.bfloat16
AXES = ("row", "col")
VMEM_LIMIT = 48 * 1024 * 1024


def dot(x, y, dims):
    return lax.dot_general(x, y, (dims, ((), ())), preferred_element_type=F32)


NN = ((1,), (0,))
NT = ((1,), (1,))
TN = ((0,), (0,))


def norm_rows(values, axis):
    centred = values - jnp.mean(values, axis=axis, keepdims=True)
    rstd = lax.rsqrt(jnp.mean(centred * centred, axis=axis, keepdims=True) + EPS)
    return centred * rstd, rstd


def norm_back(e, nhat, rstd, axis):
    first = jnp.mean(e, axis=axis, keepdims=True)
    second = jnp.mean(e * nhat, axis=axis, keepdims=True)
    return rstd * (e - first - nhat * second)


def swap_segments(v):
    lane = lax.broadcasted_iota(jnp.int32, v[0].shape, 1)
    low = lane < 64
    even = (lane // 32) % 2 == 0
    w = [None] * 4
    for m in range(2):
        w[m] = jnp.where(low, v[m], pltpu.roll(v[m + 2], 64, 1))
        w[m + 2] = jnp.where(low, pltpu.roll(v[m], 64, 1), v[m + 2])
    u = [None] * 4
    for m in (0, 2):
        u[m] = jnp.where(even, w[m], pltpu.roll(w[m + 1], 32, 1))
        u[m + 1] = jnp.where(even, pltpu.roll(w[m], 96, 1), w[m + 1])
    return u


def group(ref, t):
    return ref[:, t].reshape(128, 128)


def fetch(pairs, sems):
    copies = [pltpu.make_async_copy(far, near, sems.at[n]) for n, (far, near) in enumerate(pairs)]
    for copy in copies:
        copy.start()
    return copies


def project_kernel(contact, chain, pair_far, gain_far, w_far, chunks, zn_out, mask_out, w_t, pair, gain, w_in, left, right, sems):
    copies = fetch([(w_far, w_in), (gain_far, gain), (pair_far, pair)], sems)
    row_start = lax.axis_index("row") * 32
    col_start = lax.axis_index("col") * 32
    lane = lax.broadcasted_iota(jnp.int32, (8, 128), 1)
    sub = lax.broadcasted_iota(jnp.int32, (8, 128), 0)
    col_id = jnp.zeros((8, 128), jnp.int32)
    row_id = jnp.zeros((8, 128), jnp.int32)
    for n in range(32):
        col_id = jnp.where(lane % 32 == n, chain[col_start + n], col_id)
        row_id = jnp.where((sub == n % 8) & (lane // 32 == n // 8), chain[row_start + n], row_id)
    listed = contact[col_start // BLOCK, row_start // BLOCK]
    mask = jnp.where(row_id == col_id, 1.0, jnp.where(listed == 1, 1.0, 0.0))
    mask_out[...] = mask
    for copy in copies:
        copy.wait()
    w_t[...] = w_in[...].astype(F32).T.astype(BF16)
    for t in range(8):
        nhat, _ = norm_rows(group(pair, t).astype(F32), 1)
        zn = (nhat * gain[...]).astype(BF16)
        zn_out[t] = zn
        proj = dot(w_t[...], zn, NT)
        weight = mask[t : t + 1, :]
        left[:, t, :] = jax.nn.sigmoid(proj[128:256]) * proj[:128] * weight
        right[:, t, :] = jax.nn.sigmoid(proj[384:]) * proj[256:384] * weight
    chunks[:, 0] = left[...].astype(BF16)
    chunks[:, 1] = right[...].astype(BF16)


def product_kernel(got, keep, send, left, right, x_all):
    for hi in range(4):
        for ab, rows in enumerate((left, right)):
            u = swap_segments([got[:, hi, lo, ab].astype(F32).reshape(64, 128) for lo in range(4)])
            for m in range(4):
                rows[pl.ds(64 * m, 64), pl.ds(128 * hi, 128)] = u[m].astype(BF16)
    x_all[...] = dot(left[...], right[...], TN).reshape(8, 2, 32, 512)
    core = lax.axis_index("row") % 2
    keep[...] = x_all[:, core]
    send[...] = x_all[:, 1 - core]


def product_sum_kernel(keep, came, x_out):
    for hi in range(4):
        lanes = pl.ds(128 * hi, 128)
        u = swap_segments(
            [(keep[:, pl.ds(8 * m, 8), lanes] + came[:, pl.ds(8 * m, 8), lanes]).reshape(64, 128) for m in range(4)]
        )
        for lo in range(4):
            x_out[:, hi, lo] = u[lo].reshape(8, 8, 128).astype(BF16)


def column_of(row):
    return jnp.broadcast_to(row, (128, 128)).T


def output_kernel(
    got, zn_in, cot_far, gate_far, out_far, gain, update, dx_out, xn_out, dout_out, dgpre_out, x_all, dx_all, cot, w_gate, w_out, sems
):
    copies = fetch([(gate_far, w_gate), (out_far, w_out), (cot_far, cot)], sems)
    gain_col = column_of(gain[...])
    x_all[...] = got[...].astype(F32)
    for copy in copies:
        copy.wait()
    for t in range(8):
        xhat, xrstd = norm_rows(x_all[:, t, :], 0)
        xn = (xhat * gain_col).astype(BF16)
        outp = dot(xn, w_out[...], TN)
        gate = jax.nn.sigmoid(dot(zn_in[t], w_gate[...], NN))
        update[:, t] = (gate * outp).astype(BF16).reshape(4, 32, 128)
        dy = group(cot, t).astype(F32)
        dout = (dy * gate).astype(BF16)
        dxn = dot(w_out[...], dout, NT)
        dx_all[:, t, :] = norm_back(dxn * gain_col, xhat, xrstd, 0)
        xn_out[t] = xn
        dout_out[t] = dout
        dgpre_out[t] = (dy * outp * gate * (1.0 - gate)).astype(BF16)
    dx_out[...] = dx_all[...].astype(BF16)


def output_grads_kernel(xn, dout, dgpre, zn, w_gate, w_out, gain_in, gain, dzn, grads, gains):
    out_sum = jnp.zeros((128, 128), F32)
    gate_sum = jnp.zeros((128, 128), F32)
    for t in range(8):
        out_sum += dot(xn[t], dout[t], NN)
        gate_sum += dot(dgpre[t], zn[t], TN)
        dzn[t] = dot(dgpre[t], w_gate[...], NT)
    grads[:128] = out_sum
    grads[128:] = gate_sum
    column = jnp.sum(out_sum * w_out[...].astype(F32), axis=1, keepdims=True) / column_of(gain[...])
    row = jnp.sum(gate_sum * w_gate[...].astype(F32).T, axis=0, keepdims=True) / gain_in[...]
    first = lax.broadcasted_iota(jnp.int32, (8, 128), 0) == 0
    gains[...] = jnp.where(first, row, column.T[:8])


def back_product_kernel(got, came, left, right, out, dx_rows, d_rows):
    core = lax.axis_index("row") % 2
    for hi in range(4):
        for source, place in ((got, core), (came, 1 - core)):
            u = swap_segments([source[:, hi, lo].astype(F32).reshape(64, 128) for lo in range(4)])
            for m in range(4):
                dx_rows[:, place, m, :, pl.ds(128 * hi, 128)] = u[m].reshape(8, 8, 128)
    dx = dx_rows[...].reshape(512, 512).astype(BF16)
    d_rows[0] = dot(right[...], dx, NT)
    d_rows[1] = dot(left[...], dx, NN)
    for hi in range(4):
        for ab in range(2):
            u = swap_segments([d_rows[ab, pl.ds(64 * m, 64), pl.ds(128 * hi, 128)] for m in range(4)])
            for lo in range(4):
                out[:, hi, lo, ab] = u[lo].reshape(8, 8, 128).astype(BF16)


def input_grads_kernel(got, zn_in, mask, gain, w_t, early, early_gains, dproj_out, grads, d_left, d_right):
    total = jnp.zeros((512, 128), F32)
    d_left[...] = got[:, 0].astype(F32)
    d_right[...] = got[:, 1].astype(F32)
    for t in range(8):
        zn = zn_in[t]
        proj = dot(w_t[...], zn, NT)
        weight = mask[t : t + 1, :]
        sa = jax.nn.sigmoid(proj[128:256])
        sb = jax.nn.sigmoid(proj[384:])
        da = d_left[:, t, :] * weight * sa
        db = d_right[:, t, :] * weight * sb
        dproj = jnp.concatenate(
            [da, da * proj[:128] * (1.0 - sa), db, db * proj[256:384] * (1.0 - sb)], axis=0
        ).astype(BF16)
        dproj_out[t] = dproj
        total += dot(dproj, zn, NN)
    row = jnp.sum(total * w_t[...].astype(F32), axis=0, keepdims=True) / gain[...]
    first = lax.broadcasted_iota(jnp.int32, (8, 128), 0) == 0
    gains = early_gains[...] + jnp.where(first, row, 0.0)
    grads[...] = jnp.concatenate(
        [
            total.reshape(32, 16, 128),
            early[...].reshape(32, 8, 128),
            jnp.broadcast_to(gains[None], (32, 8, 128)),
        ],
        axis=1,
    ).astype(BF16)


def input_kernel(dproj, pair, gain, w_t, dzn_in, grad_pair):
    for t in range(8):
        nhat, rstd = norm_rows(group(pair, t).astype(F32), 1)
        dzn = dot(dproj[t], w_t[...], TN) + dzn_in[t]
        grad_pair[:, t] = norm_back(dzn * gain[...], nhat, rstd, 1).reshape(4, 32, 128)


def sum_kernel(parts, out):
    total = jnp.sum(parts[...].astype(F32), axis=0, keepdims=True)
    out[...] = jnp.broadcast_to(total, out.shape).astype(BF16)


def unpack_kernel(got, grad_in, grad_gate, grad_out, grad_gain, grad_out_gain):
    total = got[...].astype(F32)
    grad_in[...] = total[:, :16].reshape(512, 128).T
    early = total[:, 16:24].reshape(256, 128)
    grad_out[...] = early[:128]
    grad_gate[...] = early[128:].T
    grad_gain[...] = total[0, 24:25]
    grad_out_gain[...] = total[0, 25:26]


VMEM = pl.BlockSpec(memory_space=pltpu.VMEM)
SMEM = pl.BlockSpec(memory_space=pltpu.SMEM)
FAR = pl.BlockSpec(memory_space=pltpu.HBM)


def call(kernel, outs, scratch, flops, specs):
    return pl.pallas_call(
        kernel,
        out_shape=[jax.ShapeDtypeStruct(shape, dtype) for shape, dtype in outs],
        in_specs=specs,
        scratch_shapes=scratch,
        compiler_params=pltpu.CompilerParams(vmem_limit_bytes=VMEM_LIMIT),
        cost_estimate=pl.CostEstimate(flops=flops, bytes_accessed=2000000, transcendentals=0),
    )


def groups_by(place):
    found = {}
    for device in range(256):
        group_id, order = place(device // 16, device % 16)
        found.setdefault(group_id, []).append((order, device))
    return [[device for _, device in sorted(members)] for _, members in sorted(found.items())]


SAME_CORE = groups_by(lambda row, col: (row % 2, (row // 2, col)))
PLANE = groups_by(lambda row, col: ((col // 4, row // 2 % 2), (row // 4, row % 2, col % 4)))
LINE = groups_by(lambda row, col: ((row // 4, row % 2, col % 4), (col // 4, row // 2 % 2)))


def exchange(chunks, groups):
    return lax.all_to_all(chunks, AXES, 0, 0, tiled=True, axis_index_groups=groups)


def swap_cores(array):
    return lax.ppermute(array, "row", [(row, row ^ 1) for row in range(16)])


def sum_parts(parts, copies):
    (out,) = call(sum_kernel, [((copies, 32, 128), BF16)], [], 1000000, [VMEM])(parts)
    return out


def on_device(pair, cotangent, contact, chain, gain_in, output_norm_gain, w_in, w_gate, w_out):
    pair4 = pair.reshape(4, 8, 32, 128)
    cot4 = cotangent.reshape(4, 8, 32, 128)
    gain_row = gain_in.reshape(1, 128)
    out_gain_row = output_norm_gain.reshape(1, 128)
    flat = ((8, 128, 128), BF16)
    tiles = pltpu.VMEM((128, 8, 128), F32)

    chunks, zn, mask, w_t = call(
        project_kernel,
        [((128, 2, 8, 128), BF16), flat, ((8, 128), F32), ((512, 128), BF16)],
        [
            pltpu.VMEM((4, 8, 32, 128), BF16),
            pltpu.VMEM((1, 128), F32),
            pltpu.VMEM((128, 512), BF16),
            tiles,
            tiles,
            pltpu.SemaphoreType.DMA((3,)),
        ],
        134217728,
        [SMEM, SMEM, FAR, FAR, FAR],
    )(contact, chain, pair4, gain_row, w_in)
    got = exchange(chunks, SAME_CORE).reshape(8, 4, 4, 2, 8, 128)
    rows = ((256, 512), BF16)
    keep, send, left, right = call(
        product_kernel,
        [((8, 32, 512), F32), ((8, 32, 512), F32), rows, rows],
        [pltpu.VMEM((8, 2, 32, 512), F32)],
        134217728,
        [VMEM],
    )(got)
    (x_chunks,) = call(product_sum_kernel, [((8, 4, 4, 8, 128), BF16)], [], 1000000, [VMEM] * 2)(keep, swap_cores(send))
    got = exchange(x_chunks.reshape(128, 8, 128), SAME_CORE)
    update, dx_chunks, xn, dout, dgpre = call(
        output_kernel,
        [((4, 8, 32, 128), BF16), ((128, 8, 128), BF16), flat, flat, flat],
        [
            tiles,
            tiles,
            pltpu.VMEM((4, 8, 32, 128), BF16),
            pltpu.VMEM((128, 128), BF16),
            pltpu.VMEM((128, 128), BF16),
            pltpu.SemaphoreType.DMA((3,)),
        ],
        100663296,
        [VMEM, VMEM, FAR, FAR, FAR, VMEM],
    )(got, zn, cot4, w_gate, w_out, out_gain_row)
    got = exchange(dx_chunks, SAME_CORE)
    dzn, early, early_gains = call(
        output_grads_kernel,
        [((8, 128, 128), F32), ((256, 128), F32), ((8, 128), F32)],
        [],
        100663296,
        [VMEM] * 8,
    )(xn, dout, dgpre, zn, w_gate, w_out, gain_row, out_gain_row)
    came = swap_cores(got)
    blocks = (8, 4, 4, 8, 128)
    (d_chunks,) = call(
        back_product_kernel,
        [((8, 4, 4, 2, 8, 128), BF16)],
        [pltpu.VMEM((8, 2, 4, 8, 512), F32), pltpu.VMEM((2, 256, 512), F32)],
        268435456,
        [VMEM] * 4,
    )(got.reshape(blocks), came.reshape(blocks), left, right)
    got = exchange(d_chunks.reshape(128, 2, 8, 128), SAME_CORE)
    dproj, parts = call(
        input_grads_kernel,
        [((8, 512, 128), BF16), ((32, 32, 128), BF16)],
        [tiles, tiles],
        268435456,
        [VMEM] * 7,
    )(got, zn, mask, gain_row, w_t, early, early_gains)
    parts = exchange(parts, PLANE)
    (grad_pair,) = call(input_kernel, [((4, 8, 32, 128), F32)], [], 134217728, [VMEM] * 5)(dproj, pair4, gain_row, w_t, dzn)
    parts = exchange(sum_parts(parts, 8), LINE)
    parts = exchange(sum_parts(parts, 32), PLANE)
    grad_w_in, grad_w_gate, grad_w_out, grad_gain, grad_out_gain = call(
        unpack_kernel,
        [((128, 512), F32), ((128, 128), F32), ((128, 128), F32), ((1, 128), F32), ((1, 128), F32)],
        [],
        1000000,
        [VMEM],
    )(parts)
    return (
        update.reshape(32, 32, 128),
        grad_pair.reshape(32, 32, 128),
        grad_w_in,
        grad_w_gate,
        grad_w_out,
        grad_gain.reshape(128),
        grad_out_gain.reshape(128),
    )


def solution(mesh):
    return jax.shard_map(
        on_device,
        mesh=mesh,
        in_specs=(P("row", "col", None), P("row", "col", None), P(), P(), P(), P(), P(), P(), P()),
        out_specs=(P("row", "col", None), P("row", "col", None), P(), P(), P(), P(), P()),
        check_vma=False,
    )
```

```python
import jax
import jax.numpy as jnp
from jax import lax
from jax.experimental import pallas as pl
from jax.experimental.pallas import tpu as pltpu
from jax.sharding import PartitionSpec as P


BLOCK = 128
EPS = 1e-05
F32 = jnp.float32
BF16 = jnp.bfloat16
AXES = ("row", "col")
VMEM_LIMIT = 12 * 1024 * 1024


def dot(x, y, dims):
    return lax.dot_general(x, y, (dims, ((), ())), preferred_element_type=F32)


NN = ((1,), (0,))
NT = ((1,), (1,))
TN = ((0,), (0,))


def norm_rows(values, axis):
    centred = values - jnp.mean(values, axis=axis, keepdims=True)
    rstd = lax.rsqrt(jnp.mean(centred * centred, axis=axis, keepdims=True) + EPS)
    return centred * rstd, rstd


def norm_back(e, nhat, rstd, axis):
    first = jnp.mean(e, axis=axis, keepdims=True)
    second = jnp.mean(e * nhat, axis=axis, keepdims=True)
    return rstd * (e - first - nhat * second)


def swap_segments(v):
    lane = lax.broadcasted_iota(jnp.int32, v[0].shape, 1)
    low = lane < 64
    even = (lane // 32) % 2 == 0
    w = [None] * 4
    for m in range(2):
        w[m] = jnp.where(low, v[m], pltpu.roll(v[m + 2], 64, 1))
        w[m + 2] = jnp.where(low, pltpu.roll(v[m], 64, 1), v[m + 2])
    u = [None] * 4
    for m in (0, 2):
        u[m] = jnp.where(even, w[m], pltpu.roll(w[m + 1], 32, 1))
        u[m + 1] = jnp.where(even, pltpu.roll(w[m], 96, 1), w[m + 1])
    return u


def group(ref, t):
    return ref[:, t].reshape(128, 128)


def fetch(pairs, sems):
    copies = [pltpu.make_async_copy(far, near, sems.at[n]) for n, (far, near) in enumerate(pairs)]
    for copy in copies:
        copy.start()
    return copies


def project_kernel(
    pair_far, gain_far, chain_far, contact_far, w_far, chunks, zn_out, mask_out, w_t,
    left, right, pair, gain, chain, contact, w_in, sems
):
    copies = fetch(
        [(w_far, w_in), (gain_far, gain), (chain_far, chain), (contact_far, contact), (pair_far, pair)], sems
    )
    for copy in copies[:4]:
        copy.wait()
    w_t[...] = w_in[...].astype(F32).T.astype(BF16)
    row_start = lax.axis_index("row") * 32
    col_start = lax.axis_index("col") * 32
    lane = lax.broadcasted_iota(jnp.int32, (8, 128), 1)

    def chain_from(start):
        row = jnp.broadcast_to(chain[pl.ds(start // 128, 1), :], (8, 128)).astype(F32)
        return pltpu.roll(row, (128 - start % 128) % 128, 1)

    first = jnp.where(lane < 32, chain_from(col_start), 0.0)
    col_id = first + pltpu.roll(first, 32, 1) + pltpu.roll(first, 64, 1) + pltpu.roll(first, 96, 1)
    down = jnp.broadcast_to(chain_from(row_start)[:1], (128, 128)).T
    row_id = down[:8]
    for seg in range(1, 4):
        row_id = jnp.where(lane // 32 == seg, down[8 * seg : 8 * seg + 8], row_id)
    block = lax.broadcasted_iota(jnp.int32, (4, 4), 1) == row_start // BLOCK
    block = block & (lax.broadcasted_iota(jnp.int32, (4, 4), 0) == col_start // BLOCK)
    listed = jnp.sum(jnp.where(block, contact[...].astype(F32), 0.0), keepdims=True)
    mask = jnp.maximum(listed, jnp.where(row_id == col_id, 1.0, 0.0))
    mask_out[...] = mask
    copies[4].wait()
    for t in range(8):
        nhat, _ = norm_rows(group(pair, t).astype(F32), 1)
        zn = (nhat * gain[...]).astype(BF16)
        zn_out[t] = zn
        proj = dot(w_t[...], zn, NT)
        weight = mask[t : t + 1, :]
        left[:, t, :] = jax.nn.sigmoid(proj[128:256]) * proj[:128] * weight
        right[:, t, :] = jax.nn.sigmoid(proj[384:]) * proj[256:384] * weight
    chunks[:, 0] = left[...].astype(BF16)
    chunks[:, 1] = right[...].astype(BF16)


def column_of(row):
    return jnp.broadcast_to(row, (128, 128)).T


def gate_kernel(zn_in, cot, w_gate, w_out, out_gain, e_out):
    gain_col = column_of(out_gain[...])
    for t in range(8):
        gate = jax.nn.sigmoid(dot(zn_in[t], w_gate[...], NN))
        dout = (group(cot, t).astype(F32) * gate).astype(BF16)
        e_out[t] = dot(w_out[...], dout, NT) * gain_col


def slope_kernel(zn_in, w_t, mask, slopes):
    for t in range(8):
        proj = dot(w_t[...], zn_in[t], NT)
        weight = mask[t : t + 1, :]
        for n in (0, 256):
            gated = jax.nn.sigmoid(proj[n + 128 : n + 256])
            slopes[t, n : n + 128] = gated * weight
            slopes[t, n + 128 : n + 256] = gated * weight * proj[n : n + 128] * (1.0 - gated)


def product_kernel(got, keep, send, left, right, x_all):
    for hi in range(4):
        for ab, rows in enumerate((left, right)):
            u = swap_segments([got[:, hi, lo, ab].astype(F32).reshape(64, 128) for lo in range(4)])
            for m in range(4):
                rows[pl.ds(64 * m, 64), pl.ds(128 * hi, 128)] = u[m].astype(BF16)
    x_all[...] = dot(left[...], right[...], TN).reshape(8, 2, 32, 512)
    core = lax.axis_index("row") % 2
    keep[...] = x_all[:, core]
    send[...] = x_all[:, 1 - core]


def product_sum_kernel(keep, came, x_out):
    for hi in range(4):
        lanes = pl.ds(128 * hi, 128)
        u = swap_segments(
            [(keep[:, 8 * m : 8 * m + 8, lanes] + came[:, 8 * m : 8 * m + 8, lanes]).reshape(64, 128) for m in range(4)]
        )
        for lo in range(4):
            x_out[:, hi, lo] = u[lo].reshape(8, 8, 128).astype(BF16)


def output_kernel(got, e_in, out_gain, dx_out, xn_out, x_all, dx_all):
    gain_col = column_of(out_gain[...])
    x_all[...] = got[...].astype(F32)
    for t in range(8):
        xhat, xrstd = norm_rows(x_all[:, t, :], 0)
        dx_all[:, t, :] = norm_back(e_in[t], xhat, xrstd, 0)
        xn_out[t] = (xhat * gain_col).astype(BF16)
    dx_out[...] = dx_all[...].astype(BF16)


def output_grads_kernel(xn_in, cot, zn, w_gate, w_out, gain, out_gain, update, dzn, grads, gains):
    out_sum = jnp.zeros((128, 128), F32)
    gate_sum = jnp.zeros((128, 128), F32)
    for t in range(8):
        xn = xn_in[t]
        outp = dot(xn, w_out[...], TN)
        gate = jax.nn.sigmoid(dot(zn[t], w_gate[...], NN))
        dy = group(cot, t).astype(F32)
        dout = (dy * gate).astype(BF16)
        update[:, t] = (gate * outp).astype(BF16).reshape(4, 32, 128)
        dgpre = (dy * outp * gate * (1.0 - gate)).astype(BF16)
        out_sum += dot(xn, dout, NN)
        gate_sum += dot(dgpre, zn[t], TN)
        dzn[t] = dot(dgpre, w_gate[...], NT)
    grads[:128] = out_sum
    grads[128:] = gate_sum
    column = jnp.sum(out_sum * w_out[...].astype(F32), axis=1, keepdims=True) / column_of(out_gain[...])
    row = jnp.sum(gate_sum * w_gate[...].astype(F32).T, axis=0, keepdims=True) / gain[...]
    first = lax.broadcasted_iota(jnp.int32, (8, 128), 0) == 0
    gains[...] = jnp.where(first, row, column.T[:8])


def back_product_kernel(got, came, left, right, out, dx_rows, d_rows):
    core = lax.axis_index("row") % 2
    for hi in range(4):
        for source, place in ((got, core), (came, 1 - core)):
            u = swap_segments([source[:, hi, lo].astype(F32).reshape(64, 128) for lo in range(4)])
            for m in range(4):
                dx_rows[:, place, m, :, pl.ds(128 * hi, 128)] = u[m].reshape(8, 8, 128)
    dx = dx_rows[...].reshape(512, 512).astype(BF16)
    d_rows[0] = dot(right[...], dx, NT)
    d_rows[1] = dot(left[...], dx, NN)
    for hi in range(4):
        for ab in range(2):
            u = swap_segments([d_rows[ab, pl.ds(64 * m, 64), pl.ds(128 * hi, 128)] for m in range(4)])
            for lo in range(4):
                out[:, hi, lo, ab] = u[lo].reshape(8, 8, 128).astype(BF16)


def input_grads_kernel(
    got, zn, slopes, gain_far, w_t, early_far, early_gains_far, dproj_out, grads, d_left, d_right, gain, early, early_gains, sems
):
    copies = fetch([(gain_far, gain), (early_far, early), (early_gains_far, early_gains)], sems)
    total = jnp.zeros((512, 128), F32)
    d_left[...] = got[:, 0].astype(F32)
    d_right[...] = got[:, 1].astype(F32)
    for t in range(8):
        da, db = d_left[:, t, :], d_right[:, t, :]
        dproj = (jnp.concatenate([da, da, db, db], axis=0) * slopes[t]).astype(BF16)
        dproj_out[t] = dproj
        total += dot(dproj, zn[t], NN)
    for copy in copies:
        copy.wait()
    row = jnp.sum(total * w_t[...].astype(F32), axis=0, keepdims=True) / gain[...]
    first = lax.broadcasted_iota(jnp.int32, (8, 128), 0) == 0
    gains = early_gains[...] + jnp.where(first, row, 0.0)
    grads[...] = jnp.concatenate(
        [
            total.reshape(32, 16, 128),
            early[...].reshape(32, 8, 128),
            jnp.broadcast_to(gains[None], (32, 8, 128)),
        ],
        axis=1,
    ).astype(BF16)


def input_kernel(dproj, pair, gain, w_t, dzn_in, grad_pair):
    for t in range(8):
        nhat, rstd = norm_rows(group(pair, t).astype(F32), 1)
        dzn = dot(dproj[t], w_t[...], TN) + dzn_in[t]
        grad_pair[:, t] = norm_back(dzn * gain[...], nhat, rstd, 1).reshape(4, 32, 128)


def sum_kernel(parts, out):
    total = jnp.sum(parts[...].astype(F32), axis=0, keepdims=True)
    out[...] = jnp.broadcast_to(total, out.shape).astype(BF16)


def unpack_kernel(got, grad_in, grad_gate, grad_out, grad_gain, grad_out_gain):
    total = got[...].astype(F32)
    grad_in[...] = total[:, :16].reshape(512, 128).T
    early = total[:, 16:24].reshape(256, 128)
    grad_out[...] = early[:128]
    grad_gate[...] = early[128:].T
    grad_gain[...] = total[0, 24:25]
    grad_out_gain[...] = total[0, 25:26]


VMEM = pl.BlockSpec(memory_space=pltpu.VMEM)
FAR = pl.BlockSpec(memory_space=pltpu.HBM)


def far(array):
    return pltpu.with_memory_space_constraint(array, pltpu.HBM)


def call(kernel, inputs, outs, scratch, flops, far_inputs=(), far_outputs=()):
    fetched = [(inputs[n].shape, inputs[n].dtype) for n in far_inputs]
    semaphores = [pltpu.SemaphoreType.DMA((len(fetched),))] if fetched else []
    return pl.pallas_call(
        kernel,
        out_shape=[
            pltpu.HBM(shape, dtype) if n in far_outputs else jax.ShapeDtypeStruct(shape, dtype)
            for n, (shape, dtype) in enumerate(outs)
        ],
        in_specs=[FAR if n in far_inputs else VMEM for n in range(len(inputs))],
        out_specs=[VMEM] * len(outs),
        scratch_shapes=[pltpu.VMEM(shape, F32) for shape in scratch]
        + [pltpu.VMEM(shape, dtype) for shape, dtype in fetched]
        + semaphores,
        compiler_params=pltpu.CompilerParams(vmem_limit_bytes=VMEM_LIMIT),
        cost_estimate=pl.CostEstimate(flops=flops, bytes_accessed=2000000, transcendentals=0),
    )(*[far(array) if n in far_inputs else array for n, array in enumerate(inputs)])


def groups_by(place):
    found = {}
    for device in range(256):
        group_id, order = place(device // 16, device % 16)
        found.setdefault(group_id, []).append((order, device))
    return [[device for _, device in sorted(members)] for _, members in sorted(found.items())]


SAME_CORE = groups_by(lambda row, col: (row % 2, (row // 2, col)))
PLANE = groups_by(lambda row, col: ((col // 4, row // 2 % 2), (row // 4, row % 2, col % 4)))
LINE = groups_by(lambda row, col: ((row // 4, row % 2, col % 4), (col // 4, row // 2 % 2)))


def exchange(chunks, groups):
    return lax.all_to_all(chunks, AXES, 0, 0, tiled=True, axis_index_groups=groups)


def swap_cores(array):
    return lax.ppermute(array, "row", [(row, row ^ 1) for row in range(16)])


def sum_parts(parts, copies):
    return call(sum_kernel, [parts], [((copies, 32, 128), BF16)], [], 1000000)[0]


def on_device(pair, cotangent, contact, chain, gain_in, output_norm_gain, w_in, w_gate, w_out):
    pair4 = pair.reshape(4, 8, 32, 128)
    cot4 = cotangent.reshape(4, 8, 32, 128)
    gain = gain_in.reshape(1, 128)
    out_gain = output_norm_gain.reshape(1, 128)
    flat, flat_wide = ((8, 128, 128), BF16), ((8, 128, 128), F32)
    tiles, blocks = (128, 8, 128), (8, 4, 4, 8, 128)
    rows = ((256, 512), BF16)

    chunks, zn, mask, w_t = call(
        project_kernel,
        [pair4, gain, chain.reshape(4, 128), contact, w_in],
        [((128, 2, 8, 128), BF16), flat, ((8, 128), F32), ((512, 128), BF16)],
        [tiles, tiles],
        134217728,
        far_inputs=(0, 1, 2, 3, 4),
    )
    got = exchange(chunks, SAME_CORE).reshape(8, 4, 4, 2, 8, 128)
    keep, send, left, right = call(
        product_kernel,
        [got],
        [((8, 32, 512), F32), ((8, 32, 512), F32), rows, rows],
        [(8, 2, 32, 512)],
        134217728,
    )
    send, zn_then = lax.optimization_barrier((send, zn))
    (e,) = call(gate_kernel, [zn_then, cot4, w_gate, w_out, out_gain], [flat_wide], [], 67108864)
    came, e = lax.optimization_barrier((swap_cores(send), e))
    (x_chunks,) = call(product_sum_kernel, [keep, came], [(blocks, BF16)], [], 1000000)
    got = exchange(x_chunks.reshape(128, 8, 128), SAME_CORE)
    dx_chunks, xn = call(
        output_kernel, [got, e, out_gain], [((128, 8, 128), BF16), flat], [tiles, tiles], 1000000
    )
    got = exchange(dx_chunks, SAME_CORE)
    got, mask, xn = lax.optimization_barrier((got, mask, xn))
    came = swap_cores(got)
    (slopes,) = call(slope_kernel, [zn, w_t, mask], [((8, 512, 128), F32)], [], 134217728)
    update, dzn, early, early_gains = call(
        output_grads_kernel,
        [xn, cot4, zn, w_gate, w_out, gain, out_gain],
        [((4, 8, 32, 128), BF16), flat_wide, ((256, 128), F32), ((8, 128), F32)],
        [],
        134217728,
        far_outputs=(0, 1, 2, 3),
    )
    (d_chunks,) = call(
        back_product_kernel,
        [got.reshape(blocks), came.reshape(blocks), left, right],
        [((8, 4, 4, 2, 8, 128), BF16)],
        [(8, 2, 4, 8, 512), (2, 256, 512)],
        268435456,
    )
    got = exchange(d_chunks.reshape(128, 2, 8, 128), SAME_CORE)
    dproj, parts = call(
        input_grads_kernel,
        [got, zn, slopes, gain, w_t, early, early_gains],
        [((8, 512, 128), BF16), ((32, 32, 128), BF16)],
        [tiles, tiles],
        134217728,
        far_inputs=(3, 5, 6),
        far_outputs=(0, 1),
    )
    parts = exchange(parts, PLANE)
    (grad_pair,) = call(
        input_kernel, [dproj, pair4, gain, w_t, dzn], [((4, 8, 32, 128), F32)], [], 134217728
    )
    parts, grad_pair = lax.optimization_barrier((parts, grad_pair))
    parts = exchange(sum_parts(parts, 8), LINE)
    parts = exchange(sum_parts(parts, 32), PLANE)
    grad_w_in, grad_w_gate, grad_w_out, grad_gain, grad_out_gain = call(
        unpack_kernel,
        [parts],
        [((128, 512), F32), ((128, 128), F32), ((128, 128), F32), ((1, 128), F32), ((1, 128), F32)],
        [],
        1000000,
    )
    return (
        update.reshape(32, 32, 128),
        grad_pair.reshape(32, 32, 128),
        grad_w_in,
        grad_w_gate,
        grad_w_out,
        grad_gain.reshape(128),
        grad_out_gain.reshape(128),
    )


def solution(mesh):
    return jax.shard_map(
        on_device,
        mesh=mesh,
        in_specs=(P("row", "col", None), P("row", "col", None), P(), P(), P(), P(), P(), P(), P()),
        out_specs=(P("row", "col", None), P("row", "col", None), P(), P(), P(), P(), P()),
        check_vma=False,
    )
```

```python
import jax
import jax.numpy as jnp
from jax import lax
from jax.experimental import pallas as pl
from jax.experimental.pallas import tpu as pltpu
from jax.sharding import PartitionSpec as P


BLOCK = 128
EPS = 1e-05
F32 = jnp.float32
BF16 = jnp.bfloat16
AXES = ("row", "col")
VMEM_LIMIT = 12 * 1024 * 1024


def dot(x, y, dims):
    return lax.dot_general(x, y, (dims, ((), ())), preferred_element_type=F32)


NN = ((1,), (0,))
NT = ((1,), (1,))
TN = ((0,), (0,))


def norm_rows(values, axis):
    centred = values - jnp.mean(values, axis=axis, keepdims=True)
    rstd = lax.rsqrt(jnp.mean(centred * centred, axis=axis, keepdims=True) + EPS)
    return centred * rstd, rstd


def norm_back(e, nhat, rstd, axis):
    first = jnp.mean(e, axis=axis, keepdims=True)
    second = jnp.mean(e * nhat, axis=axis, keepdims=True)
    return rstd * (e - first - nhat * second)


def swap_segments(v):
    lane = lax.broadcasted_iota(jnp.int32, v[0].shape, 1)
    low = lane < 64
    even = (lane // 32) % 2 == 0
    w = [None] * 4
    for m in range(2):
        w[m] = jnp.where(low, v[m], pltpu.roll(v[m + 2], 64, 1))
        w[m + 2] = jnp.where(low, pltpu.roll(v[m], 64, 1), v[m + 2])
    u = [None] * 4
    for m in (0, 2):
        u[m] = jnp.where(even, w[m], pltpu.roll(w[m + 1], 32, 1))
        u[m + 1] = jnp.where(even, pltpu.roll(w[m], 96, 1), w[m + 1])
    return u


def group(ref, t):
    return ref[:, t].reshape(128, 128)


def fetch(pairs, sems):
    copies = [pltpu.make_async_copy(far, near, sems.at[n]) for n, (far, near) in enumerate(pairs)]
    for copy in copies:
        copy.start()
    return copies


def project_kernel(
    pair_far, gain_far, chain_far, contact_far, w_far, out_gain_far, chunks, zn_out, mask_out, w_t, gains_out,
    left, right, pair, gain, chain, contact, w_in, out_gain, sems
):
    copies = fetch(
        [
            (w_far, w_in),
            (gain_far, gain),
            (chain_far, chain),
            (contact_far, contact),
            (out_gain_far, out_gain),
            (pair_far, pair),
        ],
        sems,
    )
    for copy in copies[:5]:
        copy.wait()
    gains_out[0:8] = jnp.broadcast_to(gain[...], (8, 128))
    gains_out[8:16] = jnp.broadcast_to(out_gain[...], (8, 128))
    w_t[...] = w_in[...].astype(F32).T.astype(BF16)
    row_start = lax.axis_index("row") * 32
    col_start = lax.axis_index("col") * 32
    lane = lax.broadcasted_iota(jnp.int32, (8, 128), 1)

    def chain_from(start):
        row = jnp.broadcast_to(chain[pl.ds(start // 128, 1), :], (8, 128)).astype(F32)
        return pltpu.roll(row, (128 - start % 128) % 128, 1)

    first = jnp.where(lane < 32, chain_from(col_start), 0.0)
    col_id = first + pltpu.roll(first, 32, 1) + pltpu.roll(first, 64, 1) + pltpu.roll(first, 96, 1)
    down = jnp.broadcast_to(chain_from(row_start)[:1], (128, 128)).T
    row_id = down[:8]
    for seg in range(1, 4):
        row_id = jnp.where(lane // 32 == seg, down[8 * seg : 8 * seg + 8], row_id)
    block = lax.broadcasted_iota(jnp.int32, (4, 4), 1) == row_start // BLOCK
    block = block & (lax.broadcasted_iota(jnp.int32, (4, 4), 0) == col_start // BLOCK)
    listed = jnp.sum(jnp.where(block, contact[...].astype(F32), 0.0), keepdims=True)
    mask = jnp.maximum(listed, jnp.where(row_id == col_id, 1.0, 0.0))
    mask_out[...] = mask
    copies[5].wait()
    for t in range(8):
        nhat, _ = norm_rows(group(pair, t).astype(F32), 1)
        zn = (nhat * gain[...]).astype(BF16)
        zn_out[t] = zn
        proj = dot(w_t[...], zn, NT)
        weight = mask[t : t + 1, :]
        left[:, t, :] = jax.nn.sigmoid(proj[128:256]) * proj[:128] * weight
        right[:, t, :] = jax.nn.sigmoid(proj[384:]) * proj[256:384] * weight
    chunks[:, 0] = left[...].astype(BF16)
    chunks[:, 1] = right[...].astype(BF16)


def column_of(row):
    return jnp.broadcast_to(row, (128, 128)).T


def gate_kernel(zn_in, cot, w_gate, w_out, both_gains, e_out):
    gain_col = column_of(both_gains[8:9])
    for t in range(8):
        gate = jax.nn.sigmoid(dot(zn_in[t], w_gate[...], NN))
        dout = (group(cot, t).astype(F32) * gate).astype(BF16)
        e_out[t] = dot(w_out[...], dout, NT) * gain_col


def slope_kernel(zn_in, w_t, mask, slopes):
    for t in range(8):
        proj = dot(w_t[...], zn_in[t], NT)
        weight = mask[t : t + 1, :]
        for n in (0, 256):
            gated = jax.nn.sigmoid(proj[n + 128 : n + 256])
            slopes[t, n : n + 128] = gated * weight
            slopes[t, n + 128 : n + 256] = gated * weight * proj[n : n + 128] * (1.0 - gated)


def product_kernel(got, keep, send, left, right, x_all):
    for hi in range(4):
        for ab, rows in enumerate((left, right)):
            u = swap_segments([got[:, hi, lo, ab].astype(F32).reshape(64, 128) for lo in range(4)])
            for m in range(4):
                rows[pl.ds(64 * m, 64), pl.ds(128 * hi, 128)] = u[m].astype(BF16)
    x_all[...] = dot(left[...], right[...], TN).reshape(8, 2, 32, 512)
    core = lax.axis_index("row") % 2
    keep[...] = x_all[:, core]
    send[...] = x_all[:, 1 - core]


def product_sum_kernel(keep, came, x_out):
    for hi in range(4):
        lanes = pl.ds(128 * hi, 128)
        u = swap_segments(
            [(keep[:, 8 * m : 8 * m + 8, lanes] + came[:, 8 * m : 8 * m + 8, lanes]).reshape(64, 128) for m in range(4)]
        )
        for lo in range(4):
            x_out[:, hi, lo] = u[lo].reshape(8, 8, 128).astype(BF16)


def output_kernel(got, e_in, both_gains, dx_out, xn_out, x_all, dx_all):
    gain_col = column_of(both_gains[8:9])
    x_all[...] = got[...].astype(F32)
    for t in range(8):
        xhat, xrstd = norm_rows(x_all[:, t, :], 0)
        dx_all[:, t, :] = norm_back(e_in[t], xhat, xrstd, 0)
        xn_out[t] = (xhat * gain_col).astype(BF16)
    dx_out[...] = dx_all[...].astype(BF16)


def output_grads_kernel(xn_in, cot, zn, w_gate, w_out, both_gains, update, dzn, grads, gains):
    out_sum = jnp.zeros((128, 128), F32)
    gate_sum = jnp.zeros((128, 128), F32)
    for t in range(8):
        xn = xn_in[t]
        outp = dot(xn, w_out[...], TN)
        gate = jax.nn.sigmoid(dot(zn[t], w_gate[...], NN))
        dy = group(cot, t).astype(F32)
        dout = (dy * gate).astype(BF16)
        update[:, t] = (gate * outp).astype(BF16).reshape(4, 32, 128)
        dgpre = (dy * outp * gate * (1.0 - gate)).astype(BF16)
        out_sum += dot(xn, dout, NN)
        gate_sum += dot(dgpre, zn[t], TN)
        dzn[t] = dot(dgpre, w_gate[...], NT)
    grads[:128] = out_sum
    grads[128:] = gate_sum
    column = jnp.sum(out_sum * w_out[...].astype(F32), axis=1, keepdims=True) / column_of(both_gains[8:9])
    row = jnp.sum(gate_sum * w_gate[...].astype(F32).T, axis=0, keepdims=True) / both_gains[0:1]
    first = lax.broadcasted_iota(jnp.int32, (8, 128), 0) == 0
    gains[...] = jnp.where(first, row, column.T[:8])


def back_product_kernel(got, came, left, right, out, dx_rows, d_rows):
    core = lax.axis_index("row") % 2
    for hi in range(4):
        for source, place in ((got, core), (came, 1 - core)):
            u = swap_segments([source[:, hi, lo].astype(F32).reshape(64, 128) for lo in range(4)])
            for m in range(4):
                dx_rows[:, place, m, :, pl.ds(128 * hi, 128)] = u[m].reshape(8, 8, 128)
    dx = dx_rows[...].reshape(512, 512).astype(BF16)
    d_rows[0] = dot(right[...], dx, NT)
    d_rows[1] = dot(left[...], dx, NN)
    for hi in range(4):
        for ab in range(2):
            u = swap_segments([d_rows[ab, pl.ds(64 * m, 64), pl.ds(128 * hi, 128)] for m in range(4)])
            for lo in range(4):
                out[:, hi, lo, ab] = u[lo].reshape(8, 8, 128).astype(BF16)


def input_grads_kernel(got, zn, slopes, both_gains, w_t, early, early_gains, dproj_out, grads, d_left, d_right):
    total = jnp.zeros((512, 128), F32)
    d_left[...] = got[:, 0].astype(F32)
    d_right[...] = got[:, 1].astype(F32)
    for t in range(8):
        da, db = d_left[:, t, :], d_right[:, t, :]
        dproj = (jnp.concatenate([da, da, db, db], axis=0) * slopes[t]).astype(BF16)
        dproj_out[t] = dproj
        total += dot(dproj, zn[t], NN)
    row = jnp.sum(total * w_t[...].astype(F32), axis=0, keepdims=True) / both_gains[0:1]
    first = lax.broadcasted_iota(jnp.int32, (8, 128), 0) == 0
    gains = early_gains[...] + jnp.where(first, row, 0.0)
    grads[...] = jnp.concatenate(
        [
            total.reshape(32, 16, 128),
            early[...].reshape(32, 8, 128),
            jnp.broadcast_to(gains[None], (32, 8, 128)),
        ],
        axis=1,
    ).astype(BF16)


def input_kernel(dproj, pair, both_gains, w_t, dzn_in, grad_pair):
    for t in range(8):
        nhat, rstd = norm_rows(group(pair, t).astype(F32), 1)
        dzn = dot(dproj[t], w_t[...], TN) + dzn_in[t]
        grad_pair[:, t] = norm_back(dzn * both_gains[0:1], nhat, rstd, 1).reshape(4, 32, 128)


def sum_kernel(parts, out):
    total = jnp.sum(parts[...].astype(F32), axis=0, keepdims=True)
    out[...] = jnp.broadcast_to(total, out.shape).astype(BF16)


def unpack_kernel(got, grad_in, grad_gate, grad_out, grad_gain, grad_out_gain):
    total = got[...].astype(F32)
    grad_in[...] = total[:, :16].reshape(512, 128).T
    early = total[:, 16:24].reshape(256, 128)
    grad_out[...] = early[:128]
    grad_gate[...] = early[128:].T
    grad_gain[...] = total[0, 24:25]
    grad_out_gain[...] = total[0, 25:26]


VMEM = pl.BlockSpec(memory_space=pltpu.VMEM)
FAR = pl.BlockSpec(memory_space=pltpu.HBM)


def far(array):
    return pltpu.with_memory_space_constraint(array, pltpu.HBM)


def near(array):
    return pltpu.with_memory_space_constraint(array, pltpu.VMEM)


def call(kernel, inputs, outs, scratch, flops, far_inputs=(), far_outputs=(), near_outputs=()):
    fetched = [(inputs[n].shape, inputs[n].dtype) for n in far_inputs]
    semaphores = [pltpu.SemaphoreType.DMA((len(fetched),))] if fetched else []
    return pl.pallas_call(
        kernel,
        out_shape=[
            pltpu.HBM(shape, dtype)
            if n in far_outputs
            else pltpu.VMEM(shape, dtype)
            if n in near_outputs
            else jax.ShapeDtypeStruct(shape, dtype)
            for n, (shape, dtype) in enumerate(outs)
        ],
        in_specs=[FAR if n in far_inputs else VMEM for n in range(len(inputs))],
        out_specs=[VMEM] * len(outs),
        scratch_shapes=[pltpu.VMEM(shape, F32) for shape in scratch]
        + [pltpu.VMEM(shape, dtype) for shape, dtype in fetched]
        + semaphores,
        compiler_params=pltpu.CompilerParams(vmem_limit_bytes=VMEM_LIMIT),
        cost_estimate=pl.CostEstimate(flops=flops, bytes_accessed=2000000, transcendentals=0),
    )(*[far(array) if n in far_inputs else array for n, array in enumerate(inputs)])


def groups_by(place):
    found = {}
    for device in range(256):
        group_id, order = place(device // 16, device % 16)
        found.setdefault(group_id, []).append((order, device))
    return [[device for _, device in sorted(members)] for _, members in sorted(found.items())]


SAME_CORE = groups_by(lambda row, col: (row % 2, (row // 2, col)))
PLANE = groups_by(lambda row, col: ((col // 4, row // 2 % 2), (row // 4, row % 2, col % 4)))
LINE = groups_by(lambda row, col: ((row // 4, row % 2, col % 4), (col // 4, row // 2 % 2)))


def exchange(chunks, groups):
    return lax.all_to_all(chunks, AXES, 0, 0, tiled=True, axis_index_groups=groups)


def swap_cores(array):
    return lax.ppermute(array, "row", [(row, row ^ 1) for row in range(16)])


def sum_parts(parts, copies):
    return call(sum_kernel, [parts], [((copies, 32, 128), BF16)], [], 1000000)[0]


def on_device(pair, cotangent, contact, chain, gain_in, output_norm_gain, w_in, w_gate, w_out):
    pair4 = pair.reshape(4, 8, 32, 128)
    cot4 = cotangent.reshape(4, 8, 32, 128)
    gain = gain_in.reshape(1, 128)
    out_gain = output_norm_gain.reshape(1, 128)
    flat, flat_wide = ((8, 128, 128), BF16), ((8, 128, 128), F32)
    tiles, blocks = (128, 8, 128), (8, 4, 4, 8, 128)
    rows = ((256, 512), BF16)

    chunks, zn, mask, w_t, gains = call(
        project_kernel,
        [pair4, gain, chain.reshape(4, 128), contact, w_in, out_gain],
        [((128, 2, 8, 128), BF16), flat, ((8, 128), F32), ((512, 128), BF16), ((16, 128), F32)],
        [tiles, tiles],
        134217728,
        far_inputs=(0, 1, 2, 3, 4, 5),
        near_outputs=(4,),
    )
    got = exchange(chunks, SAME_CORE).reshape(8, 4, 4, 2, 8, 128)
    keep, send, left, right = call(
        product_kernel,
        [got],
        [((8, 32, 512), F32), ((8, 32, 512), F32), rows, rows],
        [(8, 2, 32, 512)],
        134217728,
    )
    send, zn_then = lax.optimization_barrier((send, zn))
    (e,) = call(gate_kernel, [zn_then, cot4, w_gate, w_out, gains], [flat_wide], [], 67108864)
    (slopes,) = call(slope_kernel, [zn_then, w_t, mask], [((8, 512, 128), F32)], [], 134217728)
    came, e, slopes = lax.optimization_barrier((swap_cores(send), e, slopes))
    (x_chunks,) = call(product_sum_kernel, [keep, came], [(blocks, BF16)], [], 1000000)
    got = exchange(x_chunks.reshape(128, 8, 128), SAME_CORE)
    dx_chunks, xn = call(
        output_kernel, [got, e, gains], [((128, 8, 128), BF16), flat], [tiles, tiles], 1000000
    )
    got = exchange(dx_chunks, SAME_CORE)
    got, xn = lax.optimization_barrier((got, xn))
    came = swap_cores(got)
    update, dzn, early, early_gains = call(
        output_grads_kernel,
        [xn, cot4, zn, w_gate, w_out, gains],
        [((4, 8, 32, 128), BF16), flat_wide, ((256, 128), F32), ((8, 128), F32)],
        [],
        134217728,
        far_outputs=(0, 1),
        near_outputs=(2, 3),
    )
    came, update, dzn, early, early_gains = lax.optimization_barrier((came, update, dzn, early, early_gains))
    (d_chunks,) = call(
        back_product_kernel,
        [got.reshape(blocks), came.reshape(blocks), left, right],
        [((8, 4, 4, 2, 8, 128), BF16)],
        [(8, 2, 4, 8, 512), (2, 256, 512)],
        268435456,
    )
    got = exchange(d_chunks.reshape(128, 2, 8, 128), SAME_CORE)
    dproj, parts = call(
        input_grads_kernel,
        [got, zn, slopes, gains, w_t, near(early), near(early_gains)],
        [((8, 512, 128), BF16), ((32, 32, 128), BF16)],
        [tiles, tiles],
        134217728,
        far_outputs=(0, 1),
    )
    parts = exchange(parts, PLANE)
    (grad_pair,) = call(
        input_kernel, [dproj, pair4, gains, w_t, dzn], [((4, 8, 32, 128), F32)], [], 134217728
    )
    parts, grad_pair = lax.optimization_barrier((parts, grad_pair))
    parts = exchange(sum_parts(parts, 8), LINE)
    parts = exchange(sum_parts(parts, 32), PLANE)
    grad_w_in, grad_w_gate, grad_w_out, grad_gain, grad_out_gain = call(
        unpack_kernel,
        [parts],
        [((128, 512), F32), ((128, 128), F32), ((128, 128), F32), ((1, 128), F32), ((1, 128), F32)],
        [],
        1000000,
    )
    return (
        update.reshape(32, 32, 128),
        grad_pair.reshape(32, 32, 128),
        grad_w_in,
        grad_w_gate,
        grad_w_out,
        grad_gain.reshape(128),
        grad_out_gain.reshape(128),
    )


def solution(mesh):
    return jax.shard_map(
        on_device,
        mesh=mesh,
        in_specs=(P("row", "col", None), P("row", "col", None), P(), P(), P(), P(), P(), P(), P()),
        out_specs=(P("row", "col", None), P("row", "col", None), P(), P(), P(), P(), P()),
        check_vma=False,
    )
```

```python
import jax
import jax.numpy as jnp
from jax import lax
from jax.experimental import pallas as pl
from jax.experimental.pallas import tpu as pltpu
from jax.sharding import PartitionSpec as P


BLOCK = 128
EPS = 1e-05
F32 = jnp.float32
BF16 = jnp.bfloat16
AXES = ("row", "col")
VMEM_LIMIT = 12 * 1024 * 1024


def dot(x, y, dims):
    return lax.dot_general(x, y, (dims, ((), ())), preferred_element_type=F32)


NN = ((1,), (0,))
NT = ((1,), (1,))
TN = ((0,), (0,))


def norm_rows(values, axis):
    centred = values - jnp.mean(values, axis=axis, keepdims=True)
    rstd = lax.rsqrt(jnp.mean(centred * centred, axis=axis, keepdims=True) + EPS)
    return centred * rstd, rstd


def norm_back(e, nhat, rstd, axis):
    first = jnp.mean(e, axis=axis, keepdims=True)
    second = jnp.mean(e * nhat, axis=axis, keepdims=True)
    return rstd * (e - first - nhat * second)


def swap_segments(v):
    lane = lax.broadcasted_iota(jnp.int32, v[0].shape, 1)
    low = lane < 64
    even = (lane // 32) % 2 == 0
    w = [None] * 4
    for m in range(2):
        w[m] = jnp.where(low, v[m], pltpu.roll(v[m + 2], 64, 1))
        w[m + 2] = jnp.where(low, pltpu.roll(v[m], 64, 1), v[m + 2])
    u = [None] * 4
    for m in (0, 2):
        u[m] = jnp.where(even, w[m], pltpu.roll(w[m + 1], 32, 1))
        u[m + 1] = jnp.where(even, pltpu.roll(w[m], 96, 1), w[m + 1])
    return u


def group(ref, t):
    return ref[:, t].reshape(128, 128)


def fetch(pairs, sems):
    copies = [pltpu.make_async_copy(far, near, sems.at[n]) for n, (far, near) in enumerate(pairs)]
    for copy in copies:
        copy.start()
    return copies


def project_kernel(
    pair_far, gain_far, chain_far, contact_far, w_far, out_gain_far, chunks, zn_out, mask_out, w_t, gains_out,
    left, right, pair, gain, chain, contact, w_in, out_gain, sems
):
    copies = fetch(
        [
            (w_far, w_in),
            (gain_far, gain),
            (chain_far, chain),
            (contact_far, contact),
            (out_gain_far, out_gain),
            (pair_far, pair),
        ],
        sems,
    )
    for copy in copies[:5]:
        copy.wait()
    gains_out[0:8] = jnp.broadcast_to(gain[...], (8, 128))
    gains_out[8:16] = jnp.broadcast_to(out_gain[...], (8, 128))
    w_t[...] = w_in[...].astype(F32).T.astype(BF16)
    row_start = lax.axis_index("row") * 32
    col_start = lax.axis_index("col") * 32
    lane = lax.broadcasted_iota(jnp.int32, (8, 128), 1)

    def chain_from(start):
        row = jnp.broadcast_to(chain[pl.ds(start // 128, 1), :], (8, 128)).astype(F32)
        return pltpu.roll(row, (128 - start % 128) % 128, 1)

    first = jnp.where(lane < 32, chain_from(col_start), 0.0)
    col_id = first + pltpu.roll(first, 32, 1) + pltpu.roll(first, 64, 1) + pltpu.roll(first, 96, 1)
    down = jnp.broadcast_to(chain_from(row_start)[:1], (128, 128)).T
    row_id = down[:8]
    for seg in range(1, 4):
        row_id = jnp.where(lane // 32 == seg, down[8 * seg : 8 * seg + 8], row_id)
    block = lax.broadcasted_iota(jnp.int32, (4, 4), 1) == row_start // BLOCK
    block = block & (lax.broadcasted_iota(jnp.int32, (4, 4), 0) == col_start // BLOCK)
    listed = jnp.sum(jnp.where(block, contact[...].astype(F32), 0.0), keepdims=True)
    mask = jnp.maximum(listed, jnp.where(row_id == col_id, 1.0, 0.0))
    mask_out[...] = mask
    copies[5].wait()
    for t in range(8):
        nhat, _ = norm_rows(group(pair, t).astype(F32), 1)
        zn = (nhat * gain[...]).astype(BF16)
        zn_out[t] = zn
        proj = dot(w_t[...], zn, NT)
        weight = mask[t : t + 1, :]
        left[:, t, :] = jax.nn.sigmoid(proj[128:256]) * proj[:128] * weight
        right[:, t, :] = jax.nn.sigmoid(proj[384:]) * proj[256:384] * weight
    chunks[:, 0] = left[...].astype(BF16)
    chunks[:, 1] = right[...].astype(BF16)


def column_of(row):
    return jnp.broadcast_to(row, (128, 128)).T


def gate_kernel(zn_in, cot, w_gate, w_out, both_gains, e_out):
    gain_col = column_of(both_gains[8:9])
    for t in range(8):
        gate = jax.nn.sigmoid(dot(zn_in[t], w_gate[...], NN))
        dout = (group(cot, t).astype(F32) * gate).astype(BF16)
        e_out[t] = dot(w_out[...], dout, NT) * gain_col


def slope_kernel(zn_in, w_t, mask, slopes):
    for t in range(8):
        proj = dot(w_t[...], zn_in[t], NT)
        weight = mask[t : t + 1, :]
        for n in (0, 256):
            gated = jax.nn.sigmoid(proj[n + 128 : n + 256])
            slopes[t, n : n + 128] = gated * weight
            slopes[t, n + 128 : n + 256] = gated * weight * proj[n : n + 128] * (1.0 - gated)


def product_kernel(got, keep, send, left, right, x_all):
    for hi in range(4):
        for ab, rows in enumerate((left, right)):
            u = swap_segments([got[:, hi, lo, ab].astype(F32).reshape(64, 128) for lo in range(4)])
            for m in range(4):
                rows[pl.ds(64 * m, 64), pl.ds(128 * hi, 128)] = u[m].astype(BF16)
    x_all[...] = dot(left[...], right[...], TN).reshape(8, 2, 32, 512)
    core = lax.axis_index("row") % 2
    keep[...] = x_all[:, core]
    send[...] = x_all[:, 1 - core]


def product_sum_kernel(keep, came, x_out):
    for hi in range(4):
        lanes = pl.ds(128 * hi, 128)
        u = swap_segments(
            [(keep[:, 8 * m : 8 * m + 8, lanes] + came[:, 8 * m : 8 * m + 8, lanes]).reshape(64, 128) for m in range(4)]
        )
        for lo in range(4):
            x_out[:, hi, lo] = u[lo].reshape(8, 8, 128).astype(BF16)


def output_kernel(got, e_in, both_gains, dx_out, xn_out, x_all, dx_all):
    gain_col = column_of(both_gains[8:9])
    x_all[...] = got[...].astype(F32)
    for t in range(8):
        xhat, xrstd = norm_rows(x_all[:, t, :], 0)
        dx_all[:, t, :] = norm_back(e_in[t], xhat, xrstd, 0)
        xn_out[t] = (xhat * gain_col).astype(BF16)
    dx_out[...] = dx_all[...].astype(BF16)


def output_grads_kernel(xn_in, cot, zn, w_gate, w_out, both_gains, grads, gains):
    out_sum = jnp.zeros((128, 128), F32)
    gate_sum = jnp.zeros((128, 128), F32)
    for t in range(8):
        xn = xn_in[t]
        outp = dot(xn, w_out[...], TN)
        gate = jax.nn.sigmoid(dot(zn[t], w_gate[...], NN))
        dy = group(cot, t).astype(F32)
        dout = (dy * gate).astype(BF16)
        dgpre = (dy * outp * gate * (1.0 - gate)).astype(BF16)
        out_sum += dot(xn, dout, NN)
        gate_sum += dot(dgpre, zn[t], TN)
    grads[:128] = out_sum
    grads[128:] = gate_sum
    column = jnp.sum(out_sum * w_out[...].astype(F32), axis=1, keepdims=True) / column_of(both_gains[8:9])
    row = jnp.sum(gate_sum * w_gate[...].astype(F32).T, axis=0, keepdims=True) / both_gains[0:1]
    first = lax.broadcasted_iota(jnp.int32, (8, 128), 0) == 0
    gains[...] = jnp.where(first, row, column.T[:8])


def back_product_kernel(got, came, left, right, out, dx_rows, d_rows):
    core = lax.axis_index("row") % 2
    for hi in range(4):
        for source, place in ((got, core), (came, 1 - core)):
            u = swap_segments([source[:, hi, lo].astype(F32).reshape(64, 128) for lo in range(4)])
            for m in range(4):
                dx_rows[:, place, m, :, pl.ds(128 * hi, 128)] = u[m].reshape(8, 8, 128)
    dx = dx_rows[...].reshape(512, 512).astype(BF16)
    d_rows[0] = dot(right[...], dx, NT)
    d_rows[1] = dot(left[...], dx, NN)
    for hi in range(4):
        for ab in range(2):
            u = swap_segments([d_rows[ab, pl.ds(64 * m, 64), pl.ds(128 * hi, 128)] for m in range(4)])
            for lo in range(4):
                out[:, hi, lo, ab] = u[lo].reshape(8, 8, 128).astype(BF16)


def input_grads_kernel(got, zn, slopes, both_gains, w_t, early, early_gains, dproj_out, grads, d_left, d_right):
    total = jnp.zeros((512, 128), F32)
    d_left[...] = got[:, 0].astype(F32)
    d_right[...] = got[:, 1].astype(F32)
    for t in range(8):
        da, db = d_left[:, t, :], d_right[:, t, :]
        dproj = (jnp.concatenate([da, da, db, db], axis=0) * slopes[t]).astype(BF16)
        dproj_out[t] = dproj
        total += dot(dproj, zn[t], NN)
    row = jnp.sum(total * w_t[...].astype(F32), axis=0, keepdims=True) / both_gains[0:1]
    first = lax.broadcasted_iota(jnp.int32, (8, 128), 0) == 0
    gains = early_gains[...] + jnp.where(first, row, 0.0)
    grads[...] = jnp.concatenate(
        [
            total.reshape(32, 16, 128),
            early[...].reshape(32, 8, 128),
            jnp.broadcast_to(gains[None], (32, 8, 128)),
        ],
        axis=1,
    ).astype(BF16)


def input_kernel(dproj, pair, both_gains, w_t, xn_in, cot, zn, w_gate, w_out, grad_pair, update):
    for t in range(8):
        outp = dot(xn_in[t], w_out[...], TN)
        gate = jax.nn.sigmoid(dot(zn[t], w_gate[...], NN))
        update[:, t] = (gate * outp).astype(BF16).reshape(4, 32, 128)
        dgpre = (group(cot, t).astype(F32) * outp * gate * (1.0 - gate)).astype(BF16)
        nhat, rstd = norm_rows(group(pair, t).astype(F32), 1)
        dzn = dot(dproj[t], w_t[...], TN) + dot(dgpre, w_gate[...], NT)
        grad_pair[:, t] = norm_back(dzn * both_gains[0:1], nhat, rstd, 1).reshape(4, 32, 128)


def sum_kernel(parts, out):
    total = jnp.sum(parts[...].astype(F32), axis=0, keepdims=True)
    out[...] = jnp.broadcast_to(total, out.shape).astype(BF16)


def unpack_kernel(got, grad_in, grad_gate, grad_out, grad_gain, grad_out_gain):
    total = got[...].astype(F32)
    grad_in[...] = total[:, :16].reshape(512, 128).T
    early = total[:, 16:24].reshape(256, 128)
    grad_out[...] = early[:128]
    grad_gate[...] = early[128:].T
    grad_gain[...] = total[0, 24:25]
    grad_out_gain[...] = total[0, 25:26]


VMEM = pl.BlockSpec(memory_space=pltpu.VMEM)
FAR = pl.BlockSpec(memory_space=pltpu.HBM)


def far(array):
    return pltpu.with_memory_space_constraint(array, pltpu.HBM)


def near(array):
    return pltpu.with_memory_space_constraint(array, pltpu.VMEM)


def call(kernel, inputs, outs, scratch, flops, far_inputs=(), far_outputs=(), near_outputs=()):
    fetched = [(inputs[n].shape, inputs[n].dtype) for n in far_inputs]
    semaphores = [pltpu.SemaphoreType.DMA((len(fetched),))] if fetched else []
    return pl.pallas_call(
        kernel,
        out_shape=[
            pltpu.HBM(shape, dtype)
            if n in far_outputs
            else pltpu.VMEM(shape, dtype)
            if n in near_outputs
            else jax.ShapeDtypeStruct(shape, dtype)
            for n, (shape, dtype) in enumerate(outs)
        ],
        in_specs=[FAR if n in far_inputs else VMEM for n in range(len(inputs))],
        out_specs=[VMEM] * len(outs),
        scratch_shapes=[pltpu.VMEM(shape, F32) for shape in scratch]
        + [pltpu.VMEM(shape, dtype) for shape, dtype in fetched]
        + semaphores,
        compiler_params=pltpu.CompilerParams(vmem_limit_bytes=VMEM_LIMIT),
        cost_estimate=pl.CostEstimate(flops=flops, bytes_accessed=2000000, transcendentals=0),
    )(*[far(array) if n in far_inputs else array for n, array in enumerate(inputs)])


def groups_by(place):
    found = {}
    for device in range(256):
        group_id, order = place(device // 16, device % 16)
        found.setdefault(group_id, []).append((order, device))
    return [[device for _, device in sorted(members)] for _, members in sorted(found.items())]


SAME_CORE = groups_by(lambda row, col: (row % 2, (row // 2, col)))
PLANE = groups_by(lambda row, col: ((col // 4, row // 2 % 2), (row // 4, row % 2, col % 4)))
LINE = groups_by(lambda row, col: ((row // 4, row % 2, col % 4), (col // 4, row // 2 % 2)))


def exchange(chunks, groups):
    return lax.all_to_all(chunks, AXES, 0, 0, tiled=True, axis_index_groups=groups)


def swap_cores(array):
    return lax.ppermute(array, "row", [(row, row ^ 1) for row in range(16)])


def sum_parts(parts, copies):
    return call(sum_kernel, [parts], [((copies, 32, 128), BF16)], [], 1000000)[0]


def on_device(pair, cotangent, contact, chain, gain_in, output_norm_gain, w_in, w_gate, w_out):
    pair4 = pair.reshape(4, 8, 32, 128)
    cot4 = cotangent.reshape(4, 8, 32, 128)
    gain = gain_in.reshape(1, 128)
    out_gain = output_norm_gain.reshape(1, 128)
    flat, flat_wide = ((8, 128, 128), BF16), ((8, 128, 128), F32)
    tiles, blocks = (128, 8, 128), (8, 4, 4, 8, 128)
    rows = ((256, 512), BF16)

    chunks, zn, mask, w_t, gains = call(
        project_kernel,
        [pair4, gain, chain.reshape(4, 128), contact, w_in, out_gain],
        [((128, 2, 8, 128), BF16), flat, ((8, 128), F32), ((512, 128), BF16), ((16, 128), F32)],
        [tiles, tiles],
        134217728,
        far_inputs=(0, 1, 2, 3, 4, 5),
        near_outputs=(4,),
    )
    got = exchange(chunks, SAME_CORE).reshape(8, 4, 4, 2, 8, 128)
    keep, send, left, right = call(
        product_kernel,
        [got],
        [((8, 32, 512), F32), ((8, 32, 512), F32), rows, rows],
        [(8, 2, 32, 512)],
        134217728,
    )
    send, zn_then = lax.optimization_barrier((send, zn))
    (e,) = call(gate_kernel, [zn_then, cot4, w_gate, w_out, gains], [flat_wide], [], 67108864)
    (slopes,) = call(slope_kernel, [zn_then, w_t, mask], [((8, 512, 128), F32)], [], 134217728)
    came, e, slopes = lax.optimization_barrier((swap_cores(send), e, slopes))
    (x_chunks,) = call(product_sum_kernel, [keep, came], [(blocks, BF16)], [], 1000000)
    got = exchange(x_chunks.reshape(128, 8, 128), SAME_CORE)
    dx_chunks, xn = call(
        output_kernel, [got, e, gains], [((128, 8, 128), BF16), flat], [tiles, tiles], 1000000
    )
    got = exchange(dx_chunks, SAME_CORE)
    got, xn = lax.optimization_barrier((got, xn))
    came = swap_cores(got)
    early, early_gains = call(
        output_grads_kernel,
        [xn, cot4, zn, w_gate, w_out, gains],
        [((256, 128), F32), ((8, 128), F32)],
        [],
        134217728,
        near_outputs=(0, 1),
    )
    came, early, early_gains = lax.optimization_barrier((came, early, early_gains))
    (d_chunks,) = call(
        back_product_kernel,
        [got.reshape(blocks), came.reshape(blocks), left, right],
        [((8, 4, 4, 2, 8, 128), BF16)],
        [(8, 2, 4, 8, 512), (2, 256, 512)],
        268435456,
    )
    got = exchange(d_chunks.reshape(128, 2, 8, 128), SAME_CORE)
    dproj, parts = call(
        input_grads_kernel,
        [got, zn, slopes, gains, w_t, near(early), near(early_gains)],
        [((8, 512, 128), BF16), ((32, 32, 128), BF16)],
        [tiles, tiles],
        134217728,
        far_outputs=(0, 1),
    )
    parts = exchange(parts, PLANE)
    grad_pair, update = call(
        input_kernel,
        [dproj, pair4, gains, w_t, xn, cot4, zn, w_gate, w_out],
        [((4, 8, 32, 128), F32), ((4, 8, 32, 128), BF16)],
        [],
        134217728,
    )
    parts, grad_pair, update = lax.optimization_barrier((parts, grad_pair, update))
    parts = exchange(sum_parts(parts, 8), LINE)
    parts = exchange(sum_parts(parts, 32), PLANE)
    grad_w_in, grad_w_gate, grad_w_out, grad_gain, grad_out_gain = call(
        unpack_kernel,
        [parts],
        [((128, 512), F32), ((128, 128), F32), ((128, 128), F32), ((1, 128), F32), ((1, 128), F32)],
        [],
        1000000,
    )
    return (
        update.reshape(32, 32, 128),
        grad_pair.reshape(32, 32, 128),
        grad_w_in,
        grad_w_gate,
        grad_w_out,
        grad_gain.reshape(128),
        grad_out_gain.reshape(128),
    )


def solution(mesh):
    return jax.shard_map(
        on_device,
        mesh=mesh,
        in_specs=(P("row", "col", None), P("row", "col", None), P(), P(), P(), P(), P(), P(), P()),
        out_specs=(P("row", "col", None), P("row", "col", None), P(), P(), P(), P(), P()),
        check_vma=False,
    )
```

```python
import jax
import jax.numpy as jnp
from jax import lax
from jax.experimental import pallas as pl
from jax.experimental.pallas import tpu as pltpu
from jax.sharding import PartitionSpec as P


BLOCK = 128
EPS = 1e-05
F32 = jnp.float32
BF16 = jnp.bfloat16
AXES = ("row", "col")
VMEM_LIMIT = 12 * 1024 * 1024


def dot(x, y, dims):
    return lax.dot_general(x, y, (dims, ((), ())), preferred_element_type=F32)


NN = ((1,), (0,))
NT = ((1,), (1,))
TN = ((0,), (0,))


def norm_rows(values, axis):
    centred = values - jnp.mean(values, axis=axis, keepdims=True)
    rstd = lax.rsqrt(jnp.mean(centred * centred, axis=axis, keepdims=True) + EPS)
    return centred * rstd, rstd


def norm_back(e, nhat, rstd, axis):
    first = jnp.mean(e, axis=axis, keepdims=True)
    second = jnp.mean(e * nhat, axis=axis, keepdims=True)
    return rstd * (e - first - nhat * second)


def swap_segments(v):
    lane = lax.broadcasted_iota(jnp.int32, v[0].shape, 1)
    low = lane < 64
    even = (lane // 32) % 2 == 0
    w = [None] * 4
    for m in range(2):
        w[m] = jnp.where(low, v[m], pltpu.roll(v[m + 2], 64, 1))
        w[m + 2] = jnp.where(low, pltpu.roll(v[m], 64, 1), v[m + 2])
    u = [None] * 4
    for m in (0, 2):
        u[m] = jnp.where(even, w[m], pltpu.roll(w[m + 1], 32, 1))
        u[m + 1] = jnp.where(even, pltpu.roll(w[m], 96, 1), w[m + 1])
    return u


def group(ref, t):
    return ref[:, t].reshape(128, 128)


def fetch(pairs, sems):
    copies = [pltpu.make_async_copy(far, near, sems.at[n]) for n, (far, near) in enumerate(pairs)]
    for copy in copies:
        copy.start()
    return copies


def project_kernel(
    pair_far, gain_far, chain_far, contact_far, w_far, out_gain_far, chunks, zn_out, mask_out, w_t, gains_out,
    left, right, pair, gain, chain, contact, w_in, out_gain, sems
):
    copies = fetch(
        [
            (w_far, w_in),
            (gain_far, gain),
            (chain_far, chain),
            (contact_far, contact),
            (out_gain_far, out_gain),
            (pair_far, pair),
        ],
        sems,
    )
    for copy in copies[:5]:
        copy.wait()
    gains_out[0:8] = jnp.broadcast_to(gain[...], (8, 128))
    gains_out[8:16] = jnp.broadcast_to(out_gain[...], (8, 128))
    w_t[...] = w_in[...].astype(F32).T.astype(BF16)
    row_start = lax.axis_index("row") * 32
    col_start = lax.axis_index("col") * 32
    lane = lax.broadcasted_iota(jnp.int32, (8, 128), 1)

    def chain_from(start):
        row = jnp.broadcast_to(chain[pl.ds(start // 128, 1), :], (8, 128)).astype(F32)
        return pltpu.roll(row, (128 - start % 128) % 128, 1)

    first = jnp.where(lane < 32, chain_from(col_start), 0.0)
    col_id = first + pltpu.roll(first, 32, 1) + pltpu.roll(first, 64, 1) + pltpu.roll(first, 96, 1)
    down = jnp.broadcast_to(chain_from(row_start)[:1], (128, 128)).T
    row_id = down[:8]
    for seg in range(1, 4):
        row_id = jnp.where(lane // 32 == seg, down[8 * seg : 8 * seg + 8], row_id)
    block = lax.broadcasted_iota(jnp.int32, (4, 4), 1) == row_start // BLOCK
    block = block & (lax.broadcasted_iota(jnp.int32, (4, 4), 0) == col_start // BLOCK)
    listed = jnp.sum(jnp.where(block, contact[...].astype(F32), 0.0), keepdims=True)
    mask = jnp.maximum(listed, jnp.where(row_id == col_id, 1.0, 0.0))
    mask_out[...] = mask
    copies[5].wait()
    for t in range(8):
        nhat, _ = norm_rows(group(pair, t).astype(F32), 1)
        zn = (nhat * gain[...]).astype(BF16)
        zn_out[t] = zn
        proj = dot(w_t[...], zn, NT)
        weight = mask[t : t + 1, :]
        left[:, t, :] = jax.nn.sigmoid(proj[128:256]) * proj[:128] * weight
        right[:, t, :] = jax.nn.sigmoid(proj[384:]) * proj[256:384] * weight
    chunks[:, 0] = left[...].astype(BF16)
    chunks[:, 1] = right[...].astype(BF16)


def column_of(row):
    return jnp.broadcast_to(row, (128, 128)).T


def gate_kernel(zn_in, cot, w_gate, w_out, both_gains, e_out):
    gain_col = column_of(both_gains[8:9])
    for t in range(8):
        gate = jax.nn.sigmoid(dot(zn_in[t], w_gate[...], NN))
        dout = (group(cot, t).astype(F32) * gate).astype(BF16)
        e_out[t] = dot(w_out[...], dout, NT) * gain_col


def slope_kernel(zn_in, w_t, mask, slopes):
    for t in range(8):
        proj = dot(w_t[...], zn_in[t], NT)
        weight = mask[t : t + 1, :]
        for n in (0, 256):
            gated = jax.nn.sigmoid(proj[n + 128 : n + 256])
            slopes[t, n : n + 128] = gated * weight
            slopes[t, n + 128 : n + 256] = gated * weight * proj[n : n + 128] * (1.0 - gated)


def product_kernel(got, keep, send, left, right, x_all):
    for hi in range(4):
        for ab, rows in enumerate((left, right)):
            u = swap_segments([got[:, hi, lo, ab].astype(F32).reshape(64, 128) for lo in range(4)])
            for m in range(4):
                rows[pl.ds(64 * m, 64), pl.ds(128 * hi, 128)] = u[m].astype(BF16)
    x_all[...] = dot(left[...], right[...], TN).reshape(8, 2, 32, 512)
    core = lax.axis_index("row") % 2
    keep[...] = x_all[:, core]
    send[...] = x_all[:, 1 - core].astype(BF16)


def product_sum_kernel(keep, came, x_out):
    both = keep[...] + came[...].astype(F32)
    for hi in range(4):
        u = swap_segments([both[:, 8 * m : 8 * m + 8, 128 * hi : 128 * hi + 128].reshape(64, 128) for m in range(4)])
        for lo in range(4):
            x_out[:, hi, lo] = u[lo].reshape(8, 8, 128).astype(BF16)


def output_kernel(got, e_in, both_gains, dx_out, xn_out, x_all, dx_all):
    gain_col = column_of(both_gains[8:9])
    x_all[...] = got[...].astype(F32)
    for t in range(8):
        xhat, xrstd = norm_rows(x_all[:, t, :], 0)
        dx_all[:, t, :] = norm_back(e_in[t], xhat, xrstd, 0)
        xn_out[t] = (xhat * gain_col).astype(BF16)
    dx_out[...] = dx_all[...].astype(BF16)


def output_grads_kernel(xn_in, cot, zn, w_gate, w_out, both_gains, grads, gains):
    out_sum = jnp.zeros((128, 128), F32)
    gate_sum = jnp.zeros((128, 128), F32)
    for t in range(8):
        xn = xn_in[t]
        outp = dot(xn, w_out[...], TN)
        gate = jax.nn.sigmoid(dot(zn[t], w_gate[...], NN))
        dy = group(cot, t).astype(F32)
        dout = (dy * gate).astype(BF16)
        dgpre = (dy * outp * gate * (1.0 - gate)).astype(BF16)
        out_sum += dot(xn, dout, NN)
        gate_sum += dot(dgpre, zn[t], TN)
    grads[:128] = out_sum
    grads[128:] = gate_sum
    column = jnp.sum(out_sum * w_out[...].astype(F32), axis=1, keepdims=True) / column_of(both_gains[8:9])
    row = jnp.sum(gate_sum * w_gate[...].astype(F32).T, axis=0, keepdims=True) / both_gains[0:1]
    first = lax.broadcasted_iota(jnp.int32, (8, 128), 0) == 0
    gains[...] = jnp.where(first, row, column.T[:8])


def back_product_kernel(got, came, left, right, out, dx_rows, d_rows):
    core = lax.axis_index("row") % 2
    for hi in range(4):
        for source, place in ((got, core), (came, 1 - core)):
            u = swap_segments([source[:, hi, lo].astype(F32).reshape(64, 128) for lo in range(4)])
            for m in range(4):
                dx_rows[:, place, m, :, pl.ds(128 * hi, 128)] = u[m].reshape(8, 8, 128)
    dx = dx_rows[...].reshape(512, 512).astype(BF16)
    d_rows[0] = dot(right[...], dx, NT)
    d_rows[1] = dot(left[...], dx, NN)
    for hi in range(4):
        for ab in range(2):
            u = swap_segments([d_rows[ab, pl.ds(64 * m, 64), pl.ds(128 * hi, 128)] for m in range(4)])
            for lo in range(4):
                out[:, hi, lo, ab] = u[lo].reshape(8, 8, 128).astype(BF16)


def input_grads_kernel(got, zn, slopes, both_gains, w_t, early, early_gains, dproj_out, grads, d_left, d_right):
    total = jnp.zeros((512, 128), F32)
    d_left[...] = got[:, 0].astype(F32)
    d_right[...] = got[:, 1].astype(F32)
    for t in range(8):
        da, db = d_left[:, t, :], d_right[:, t, :]
        dproj = (jnp.concatenate([da, da, db, db], axis=0) * slopes[t]).astype(BF16)
        dproj_out[t] = dproj
        total += dot(dproj, zn[t], NN)
    row = jnp.sum(total * w_t[...].astype(F32), axis=0, keepdims=True) / both_gains[0:1]
    first = lax.broadcasted_iota(jnp.int32, (8, 128), 0) == 0
    gains = early_gains[...] + jnp.where(first, row, 0.0)
    grads[...] = jnp.concatenate(
        [
            total.reshape(32, 16, 128),
            early[...].reshape(32, 8, 128),
            jnp.broadcast_to(gains[None], (32, 8, 128)),
        ],
        axis=1,
    ).astype(BF16)


def input_kernel(dproj, pair, both_gains, w_t, xn_in, cot, zn, w_gate, w_out, grad_pair, update):
    for t in range(8):
        outp = dot(xn_in[t], w_out[...], TN)
        gate = jax.nn.sigmoid(dot(zn[t], w_gate[...], NN))
        update[:, t] = (gate * outp).astype(BF16).reshape(4, 32, 128)
        dgpre = (group(cot, t).astype(F32) * outp * gate * (1.0 - gate)).astype(BF16)
        nhat, rstd = norm_rows(group(pair, t).astype(F32), 1)
        dzn = dot(dproj[t], w_t[...], TN) + dot(dgpre, w_gate[...], NT)
        grad_pair[:, t] = norm_back(dzn * both_gains[0:1], nhat, rstd, 1).reshape(4, 32, 128)


def sum_kernel(parts, out):
    total = jnp.sum(parts[...].astype(F32), axis=0, keepdims=True)
    out[...] = jnp.broadcast_to(total, out.shape).astype(BF16)


def unpack_kernel(got, grad_in, grad_gate, grad_out, grad_gain, grad_out_gain):
    total = got[...].astype(F32)
    grad_in[...] = total[:, :16].reshape(512, 128).T
    early = total[:, 16:24].reshape(256, 128)
    grad_out[...] = early[:128]
    grad_gate[...] = early[128:].T
    grad_gain[...] = total[0, 24:25]
    grad_out_gain[...] = total[0, 25:26]


VMEM = pl.BlockSpec(memory_space=pltpu.VMEM)
FAR = pl.BlockSpec(memory_space=pltpu.HBM)


def far(array):
    return pltpu.with_memory_space_constraint(array, pltpu.HBM)


def near(array):
    return pltpu.with_memory_space_constraint(array, pltpu.VMEM)


def call(kernel, inputs, outs, scratch, flops, far_inputs=(), far_outputs=(), near_outputs=()):
    fetched = [(inputs[n].shape, inputs[n].dtype) for n in far_inputs]
    semaphores = [pltpu.SemaphoreType.DMA((len(fetched),))] if fetched else []
    return pl.pallas_call(
        kernel,
        out_shape=[
            pltpu.HBM(shape, dtype)
            if n in far_outputs
            else pltpu.VMEM(shape, dtype)
            if n in near_outputs
            else jax.ShapeDtypeStruct(shape, dtype)
            for n, (shape, dtype) in enumerate(outs)
        ],
        in_specs=[FAR if n in far_inputs else VMEM for n in range(len(inputs))],
        out_specs=[VMEM] * len(outs),
        scratch_shapes=[pltpu.VMEM(shape, F32) for shape in scratch]
        + [pltpu.VMEM(shape, dtype) for shape, dtype in fetched]
        + semaphores,
        compiler_params=pltpu.CompilerParams(vmem_limit_bytes=VMEM_LIMIT),
        cost_estimate=pl.CostEstimate(flops=flops, bytes_accessed=2000000, transcendentals=0),
    )(*[far(array) if n in far_inputs else array for n, array in enumerate(inputs)])


def groups_by(place):
    found = {}
    for device in range(256):
        group_id, order = place(device // 16, device % 16)
        found.setdefault(group_id, []).append((order, device))
    return [[device for _, device in sorted(members)] for _, members in sorted(found.items())]


SAME_CORE = groups_by(lambda row, col: (row % 2, (row // 2, col)))
PLANE = groups_by(lambda row, col: ((col // 4, row // 2 % 2), (row // 4, row % 2, col % 4)))
LINE = groups_by(lambda row, col: ((row // 4, row % 2, col % 4), (col // 4, row // 2 % 2)))


def exchange(chunks, groups):
    return lax.all_to_all(chunks, AXES, 0, 0, tiled=True, axis_index_groups=groups)


def swap_cores(array):
    return lax.ppermute(array, "row", [(row, row ^ 1) for row in range(16)])


def sum_parts(parts, copies):
    return call(sum_kernel, [parts], [((copies, 32, 128), BF16)], [], 1000000)[0]


def on_device(pair, cotangent, contact, chain, gain_in, output_norm_gain, w_in, w_gate, w_out):
    pair4 = pair.reshape(4, 8, 32, 128)
    cot4 = cotangent.reshape(4, 8, 32, 128)
    gain = gain_in.reshape(1, 128)
    out_gain = output_norm_gain.reshape(1, 128)
    flat, flat_wide = ((8, 128, 128), BF16), ((8, 128, 128), F32)
    tiles, blocks = (128, 8, 128), (8, 4, 4, 8, 128)
    rows = ((256, 512), BF16)

    chunks, zn, mask, w_t, gains = call(
        project_kernel,
        [pair4, gain, chain.reshape(4, 128), contact, w_in, out_gain],
        [((128, 2, 8, 128), BF16), flat, ((8, 128), F32), ((512, 128), BF16), ((16, 128), F32)],
        [tiles, tiles],
        134217728,
        far_inputs=(0, 1, 2, 3, 4, 5),
        near_outputs=(4,),
    )
    got = exchange(chunks, SAME_CORE).reshape(8, 4, 4, 2, 8, 128)
    keep, send, left, right = call(
        product_kernel,
        [got],
        [((8, 32, 512), F32), ((8, 32, 512), BF16), rows, rows],
        [(8, 2, 32, 512)],
        134217728,
    )
    send, zn_then = lax.optimization_barrier((send, zn))
    (e,) = call(gate_kernel, [zn_then, cot4, w_gate, w_out, gains], [flat_wide], [], 67108864)
    (slopes,) = call(slope_kernel, [zn_then, w_t, mask], [((8, 512, 128), F32)], [], 134217728)
    came, e, slopes = lax.optimization_barrier((swap_cores(send), e, slopes))
    (x_chunks,) = call(product_sum_kernel, [keep, came], [(blocks, BF16)], [], 1000000)
    got = exchange(x_chunks.reshape(128, 8, 128), SAME_CORE)
    dx_chunks, xn = call(
        output_kernel, [got, e, gains], [((128, 8, 128), BF16), flat], [tiles, tiles], 1000000
    )
    got = exchange(dx_chunks, SAME_CORE)
    got, xn = lax.optimization_barrier((got, xn))
    came = swap_cores(got)
    early, early_gains = call(
        output_grads_kernel,
        [xn, cot4, zn, w_gate, w_out, gains],
        [((256, 128), F32), ((8, 128), F32)],
        [],
        134217728,
        near_outputs=(0, 1),
    )
    came, early, early_gains = lax.optimization_barrier((came, early, early_gains))
    (d_chunks,) = call(
        back_product_kernel,
        [got.reshape(blocks), came.reshape(blocks), left, right],
        [((8, 4, 4, 2, 8, 128), BF16)],
        [(8, 2, 4, 8, 512), (2, 256, 512)],
        268435456,
    )
    got = exchange(d_chunks.reshape(128, 2, 8, 128), SAME_CORE)
    dproj, parts = call(
        input_grads_kernel,
        [got, zn, slopes, gains, w_t, near(early), near(early_gains)],
        [((8, 512, 128), BF16), ((32, 32, 128), BF16)],
        [tiles, tiles],
        134217728,
        far_outputs=(0, 1),
    )
    parts = exchange(parts, PLANE)
    grad_pair, update = call(
        input_kernel,
        [dproj, pair4, gains, w_t, xn, cot4, zn, w_gate, w_out],
        [((4, 8, 32, 128), F32), ((4, 8, 32, 128), BF16)],
        [],
        134217728,
    )
    parts, grad_pair, update = lax.optimization_barrier((parts, grad_pair, update))
    parts = exchange(sum_parts(parts, 8), LINE)
    parts = exchange(sum_parts(parts, 32), PLANE)
    grad_w_in, grad_w_gate, grad_w_out, grad_gain, grad_out_gain = call(
        unpack_kernel,
        [parts],
        [((128, 512), F32), ((128, 128), F32), ((128, 128), F32), ((1, 128), F32), ((1, 128), F32)],
        [],
        1000000,
    )
    return (
        update.reshape(32, 32, 128),
        grad_pair.reshape(32, 32, 128),
        grad_w_in,
        grad_w_gate,
        grad_w_out,
        grad_gain.reshape(128),
        grad_out_gain.reshape(128),
    )


def solution(mesh):
    return jax.shard_map(
        on_device,
        mesh=mesh,
        in_specs=(P("row", "col", None), P("row", "col", None), P(), P(), P(), P(), P(), P(), P()),
        out_specs=(P("row", "col", None), P("row", "col", None), P(), P(), P(), P(), P()),
        check_vma=False,
    )
```
